128 devices in a mesh: dom: 16 (over z, y), sub: 8 (over x, core).
Axes of the slice: x: 4, y: 4, z: 4, core: 2. Of those that a mesh axis runs over, the one named last changes fastest.
Arguments:
- a_vals: bfloat16 [4096, 4, 128, 128], P(('dom', 'sub')), may hold values from -0.5 to 8.5, as said below
- a_cols: int32 [4096, 4], P(('dom', 'sub')), may hold values from 0 to 47, as said below
- send_rows: int32 [128, 2, 8], P(('dom', 'sub')), may hold values from 0 to 31, as said below
- tentative: bfloat16 [4096, 128, 128], P(('dom', 'sub')), may hold values from -0.046875 to 0.046875
- p_cols: int32 [4096, 4], P(('dom', 'sub')), may hold values from 0 to 5, as said below
- ap_cols: int32 [4096, 4, 4], P(('dom', 'sub')), may hold values from 0 to 9, as said below
Outputs:
- coarse_matrix: float32 [4096, 1792], P(('dom', 'sub'))
The draws below stay inside these ranges and needn't reach their ends.
Inputs may be any that keep to these rules, and one draw needn't show every extreme that they name: `send_rows`: the two lists of a partition name 16 distinct local tile rows. `a_cols`: entry 0 of a tile row's list is the row itself and a row's entries are distinct. Values below 32 are own rows; 32 + j is the j-th row of the upward list of the partition one slab lower with the same sub index, 40 + j the j-th row of the downward list of the partition one slab higher. Partitions of the first and last slab reference no missing neighbour. p_cols[i, m] = (slab of the row referenced by a_cols[i, m] - slab of i + 1) * 2 + the aggregate of that row within its slab; aggregates of a slab may gather rows of all its partitions. ap_cols[i, k, m] = p_cols[r, m] + (slab of r - slab of i + 1) * 2, where r is the row referenced by a_cols[i, k]. `a_vals`: the diagonal entries of each row's first tile are positive.
All inputs are finite; a program needn't handle non-finite values.
Results may differ from the reference program's by a relative error of at most 0.0007.
Values may be sent and summed in bfloat16 or wider, within the bound.
A program may use at most 128 MiB of HBM per device.

```python
import jax
import jax.numpy as jnp
from jax import lax

B = 128
K = 4
TR = 32
NCG = 2
GD = 8
SUBS = 8
PARTS_SIZE = 128
ROWS = 4096
AGG_ROWS = 128
N_DOM = 16
N_SUB = 8


def pick_rows(source, chosen_rows):
    return source[chosen_rows]


def structure(key):
    key = jax.random.fold_in(key, 101)
    key_lists, key_cols, key_aggs = jax.random.split(key, 3)
    ext_count = TR + 2 * GD
    scores = jax.random.randint(key_lists, (PARTS_SIZE, TR), 0, 1 << 20) * TR + jnp.arange(TR, dtype=jnp.int32)
    ranking = jnp.argsort(scores, axis=1).astype(jnp.int32)
    outgoing = jnp.stack([ranking[:, :GD], ranking[:, TR - GD:]], 1)
    positions = jnp.arange(ext_count, dtype=jnp.int32)
    slab_of = (jnp.arange(PARTS_SIZE, dtype=jnp.int32) // SUBS)[:, None, None]
    random_ext = jax.random.randint(key_cols, (PARTS_SIZE, TR, ext_count), 0, 1 << 20) * ext_count + positions
    own_row = positions[None, None, :] == jnp.arange(TR, dtype=jnp.int32)[None, :, None]
    no_lower = (slab_of == 0) & (positions >= TR) & (positions < TR + GD)
    no_upper = (slab_of == PARTS_SIZE // SUBS - 1) & (positions >= TR + GD)
    random_ext = jnp.where(own_row | no_lower | no_upper, -1 - positions, random_ext)
    chosen = lax.top_k(random_ext, K - 1)[1].astype(jnp.int32)
    self_col = jnp.broadcast_to(jnp.arange(TR, dtype=jnp.int32)[None, :, None], (PARTS_SIZE, TR, 1))
    a_cols = jnp.concatenate([self_col, chosen], 2)
    aggregate = jax.random.randint(key_aggs, (PARTS_SIZE, TR), 0, NCG).astype(jnp.int32)
    part_ids = jnp.arange(PARTS_SIZE, dtype=jnp.int32)
    below_part = jnp.maximum(part_ids - SUBS, 0)
    above_part = jnp.minimum(part_ids + SUBS, PARTS_SIZE - 1)
    ext_slots = jnp.concatenate([aggregate + NCG, jax.vmap(pick_rows)(aggregate[below_part], outgoing[below_part, 1]), jax.vmap(pick_rows)(aggregate[above_part], outgoing[above_part, 0]) + 2 * NCG], 1)
    p_cols = jax.vmap(pick_rows)(ext_slots, a_cols)
    ext_pcols = jnp.concatenate([p_cols + NCG, jax.vmap(pick_rows)(p_cols[below_part], outgoing[below_part, 1]), jax.vmap(pick_rows)(p_cols[above_part], outgoing[above_part, 0]) + 2 * NCG], 1)
    ap_cols = jax.vmap(pick_rows)(ext_pcols, a_cols)
    return (outgoing, a_cols, p_cols, ap_cols)


def draw_send_rows(key, part):
    shared = structure(key)
    key = jax.random.fold_in(key, 1)
    return shared[0]


def draw_a_cols(key, part):
    shared = structure(key)
    key = jax.random.fold_in(key, 2)
    return shared[1].reshape(PARTS_SIZE * TR, K)


def draw_p_cols(key, part):
    shared = structure(key)
    key = jax.random.fold_in(key, 3)
    return shared[2].reshape(PARTS_SIZE * TR, K)


def draw_ap_cols(key, part):
    shared = structure(key)
    key = jax.random.fold_in(key, 4)
    return shared[3].reshape(PARTS_SIZE * TR, K, K)


def draw_a_vals(key, part):
    key = jax.random.fold_in(key, 7)
    key_noise, key_diag = jax.random.split(key)
    shape_all = (PARTS_SIZE * TR, K, B, B)
    noise = jnp.clip(jax.random.normal(key_noise, shape_all, jnp.float32), -4.0, 4.0) * 0.08
    diagonal = jax.random.uniform(key_diag, (PARTS_SIZE * TR, B), jnp.float32, 2.0, 4.0)
    leading = noise[:, 0] + diagonal[:, :, None] * jnp.eye(B, dtype=jnp.float32)
    return jnp.concatenate([leading[:, None], noise[:, 1:]], 1).astype(jnp.bfloat16)


def level_of(rng, shape, shards, smallest, high):
    def one(position, blocks):
        heights = jax.random.uniform(jax.random.fold_in(jax.random.fold_in(rng, 6), position), (blocks,), jnp.float32, smallest / len(shards), high / len(shards))
        return jnp.repeat(jnp.exp(heights), shape[position] // blocks).reshape((-1,) + (1,) * (len(shape) - position - 1))

    level = one(*shards[0])
    for cut in shards[1:]:
        level = level * one(*cut)
    return level


def bell_draw(rng, dims, spread, bound, cuts=(), kind=jnp.bfloat16):
    drawn = spread * jax.random.normal(rng, dims, jnp.float32)
    if cuts:
        drawn = drawn * level_of(rng, dims, cuts, -0.22, 0.18)
    return jnp.clip(drawn, -bound, bound).astype(kind)


def setup_inputs(seed: int = 0) -> dict:
    splits = jax.random.split(jax.random.key(seed), 7)
    a_vals = draw_a_vals(jax.random.fold_in(splits[6], 71), 0)
    a_cols = draw_a_cols(jax.random.fold_in(splits[6], 71), 0)
    send_rows = draw_send_rows(jax.random.fold_in(splits[6], 71), 0)
    tentative = bell_draw(splits[3], (ROWS, B, B), (B * AGG_ROWS) ** -0.5, 0.046875, ((0, 128),))
    p_cols = draw_p_cols(jax.random.fold_in(splits[6], 71), 0)
    ap_cols = draw_ap_cols(jax.random.fold_in(splits[6], 71), 0)
    return {"a_vals": a_vals, "a_cols": a_cols, "send_rows": send_rows, "tentative": tentative, "p_cols": p_cols, "ap_cols": ap_cols}


OMEGA = 0.6


def neighbours(source, send_rows, part_index):
    total = source.shape[0]
    below_part = jnp.maximum(part_index - N_SUB, 0)
    above_part = jnp.minimum(part_index + N_SUB, total - 1)
    from_lower = source[below_part][send_rows[below_part, 1]]
    from_upper = source[above_part][send_rows[above_part, 0]]
    from_lower = jnp.where(part_index >= N_SUB, from_lower, jnp.zeros_like(from_lower))
    from_upper = jnp.where(part_index + N_SUB < total, from_upper, jnp.zeros_like(from_upper))
    return jnp.concatenate([source[part_index], from_lower, from_upper], 0)


def reference(a_vals, a_cols, send_rows, tentative, p_cols, ap_cols):
    partitions = N_DOM * N_SUB
    tile_vals = a_vals.reshape(partitions, TR, K, B, B)
    col_list = a_cols.reshape(partitions, TR, K)
    tentative_rows = tentative.reshape(partitions, TR, B, B)
    row_slots = p_cols.reshape(partitions, TR, K)
    col_slots = ap_cols.reshape(partitions, TR, K * K)
    first_tile = (jnp.arange(K) == 0)[None, :, None, None]

    def smooth_one(part_index):
        extended = neighbours(tentative_rows, send_rows, part_index)
        gathered = extended[col_list[part_index]]
        product = jnp.einsum('tkxz,tkzy->tkxy', tile_vals[part_index].astype(jnp.float32), gathered.astype(jnp.float32))
        inverse = 1.0 / jnp.diagonal(tile_vals[part_index][:, 0].astype(jnp.float32), axis1=1, axis2=2)
        leading = jnp.where(first_tile, tentative_rows[part_index][:, None].astype(jnp.float32), jnp.zeros((), jnp.float32))
        return (leading - OMEGA * inverse[:, None, :, None] * product).astype(jnp.bfloat16)

    part_ids = jnp.arange(partitions, dtype=jnp.int32)
    smoothed = lax.map(smooth_one, part_ids)
    col_ids = jnp.arange(5 * NCG, dtype=jnp.int32)
    row_ids = jnp.arange(3 * NCG, dtype=jnp.int32)

    def coarse_one(part_index):
        extended = neighbours(smoothed, send_rows, part_index)
        fetched = extended[col_list[part_index]]
        products = jnp.einsum('tkxz,tkmzy->tkmxy', tile_vals[part_index].astype(jnp.float32), fetched.astype(jnp.float32))
        products = products.reshape(TR, K * K, B, B)
        pick_cols = (col_slots[part_index][:, :, None] == col_ids).astype(jnp.float32)
        placed = jnp.einsum('tnc,tnxy->txcy', pick_cols, products, precision=lax.Precision.HIGHEST)
        placed = placed.reshape(TR, B, 5 * NCG * B).astype(jnp.bfloat16)
        weighted = jnp.einsum('tmzx,tzc->tmxc', smoothed[part_index].astype(jnp.float32), placed.astype(jnp.float32))
        pick_rows = (row_slots[part_index][:, :, None] == row_ids).astype(jnp.float32)
        partial_value = jnp.einsum('tmr,tmxc->rxc', pick_rows, weighted, precision=lax.Precision.HIGHEST)
        return partial_value.reshape(3, NCG * B, 5 * NCG * B)

    partials = lax.map(coarse_one, part_ids)
    coarse_width = NCG * B
    zero_block = jnp.zeros((N_SUB, coarse_width, 5 * coarse_width), jnp.float32)
    from_lower = jnp.concatenate([zero_block, partials[:-N_SUB, 2]], 0)
    from_upper = jnp.concatenate([partials[N_SUB:, 0], zero_block], 0)
    coarse_band = (jnp.pad(from_lower, ((0, 0), (0, 0), (0, 2 * coarse_width)))
                   + jnp.pad(partials[:, 1], ((0, 0), (0, 0), (coarse_width, coarse_width)))
                   + jnp.pad(from_upper, ((0, 0), (0, 0), (2 * coarse_width, 0))))
    summed = coarse_band.reshape(N_DOM, N_SUB, coarse_width, 7 * coarse_width).sum(axis=1)
    return summed.reshape(N_DOM * coarse_width, 7 * coarse_width)
```

```python
import jax
import jax.numpy as jnp
from jax import lax
from jax.experimental import pallas as pl
from jax.experimental.pallas import tpu as pltpu
from jax.sharding import PartitionSpec as P

B = 128
K = 4
TR = 32
NCG = 2
GD = 8
G = NCG * B
OMEGA = 0.6
F32 = jnp.float32
BF16 = jnp.bfloat16
MESH = pl.DeviceIdType.MESH


def smooth_tiles(a_v, t_ext, cols_ref, row, eye):
    diagonal = jnp.sum(jnp.where(eye, a_v[row, 0].astype(F32), 0.0), axis=1, keepdims=True)
    weight = OMEGA * (1.0 / diagonal)
    tiles = []
    for m in range(K):
        product = jnp.dot(a_v[row, m], t_ext[cols_ref[row, m]], preferred_element_type=F32)
        value = weight * product
        value = t_ext[row].astype(F32) - value if m == 0 else -value
        tiles.append(value.astype(BF16))
    return tiles


def slot_tile(tiles, factor, slot):
    total = None
    for m in range(K):
        if m == 0 and slot // NCG != 1:
            continue
        term = tiles[m] * factor(m, slot)
        total = term if total is None else total + term
    return total


def kernel(
    a_hbm, cols_ref, lists_ref, t_hbm, slots_ref, out_ref,
    a_v, t_own, t_ext, t_send, s_send, s_halo, pc_send, pc_halo,
    p_all, p_t, ap, part, core_in, q, x_in, x_fwd, y_in,
    load_sem, t_ssem, t_rsem, s_ssem, s_rsem, pc_ssem, pc_rsem,
    c_ssem, c_rsem, x_ssem, x_rsem, y_ssem, y_rsem,
):
    dom, sub = lax.axis_index("dom"), lax.axis_index("sub")
    n_dom = lax.axis_size("dom")
    up, down = lax.rem(dom + 1, n_dom), lax.rem(dom + n_dom - 1, n_dom)
    x, core = sub // 2, lax.rem(sub, 2)
    xa = x + 1 - 2 * lax.rem(x, 2)
    xb = 3 - x
    xo = lax.rem(x + 2, 4)
    to_up, to_down = (up, sub), (down, sub)
    to_core = (dom, 2 * x + 1 - core)
    to_a, to_b = (dom, 2 * xa + core), (dom, 2 * xb + core)

    load_own = pltpu.make_async_copy(t_hbm, t_own, load_sem.at[0])
    load_ext = pltpu.make_async_copy(t_hbm, t_ext.at[pl.ds(0, TR)], load_sem.at[1])
    load_a = pltpu.make_async_copy(a_hbm, a_v, load_sem.at[2])
    load_own.start()
    load_a.start()
    load_ext.start()

    barrier = pltpu.get_barrier_semaphore()
    for device in (to_up, to_down, to_core, to_a, to_b):
        pl.semaphore_signal(barrier, inc=1, device_id=device, device_id_type=MESH)

    for side in range(2):
        for j in range(GD):
            row = lists_ref[side, j]
            for m in range(K):
                pc_send[side, m, j : j + 1, :] = jnp.full((1, B), slots_ref[row, m], jnp.int32)

    def remote(src, dst, ssem, rsem, device):
        return pltpu.make_async_remote_copy(
            src_ref=src, dst_ref=dst, send_sem=ssem, recv_sem=rsem,
            device_id=device, device_id_type=MESH,
        )

    load_own.wait()

    def gather_row(j, carry):
        for side in range(2):
            t_send[side, j] = t_own[lists_ref[side, j]]
        return carry

    lax.fori_loop(0, GD, gather_row, 0)
    pl.semaphore_wait(barrier, 5)

    t_up = remote(t_send.at[1], t_ext.at[pl.ds(TR, GD)], t_ssem.at[0], t_rsem.at[0], to_up)
    t_down = remote(t_send.at[0], t_ext.at[pl.ds(TR + GD, GD)], t_ssem.at[1], t_rsem.at[1], to_down)
    t_up.start()
    t_down.start()
    pc_up = remote(pc_send.at[1], pc_halo.at[0], pc_ssem.at[0], pc_rsem.at[0], to_up)
    pc_down = remote(pc_send.at[0], pc_halo.at[1], pc_ssem.at[1], pc_rsem.at[1], to_down)
    pc_up.start()
    pc_down.start()

    empty = jnp.zeros((B, G), BF16)

    def clear(first, groups):
        def body(j, carry):
            for g in groups:
                p_all[first + j, g] = empty
            return carry

        return body

    lax.fori_loop(0, TR, clear(0, (0, 4)), 0)
    lax.fori_loop(0, GD, clear(TR, (3, 4)), 0)
    lax.fori_loop(0, GD, clear(TR + GD, (0, 1)), 0)

    load_a.wait()
    load_ext.wait()
    t_up.wait_recv()
    t_down.wait_recv()

    eye = lax.broadcasted_iota(jnp.int32, (B, B), 0) == lax.broadcasted_iota(jnp.int32, (B, B), 1)

    def send_row(j, carry):
        for side in range(2):
            tiles = smooth_tiles(a_v, t_ext, cols_ref, lists_ref[side, j], eye)
            for m in range(K):
                s_send[side, j, m] = tiles[m]
            region = GD * (1 - side)
            remote(
                s_send.at[side, j], s_halo.at[region + j], s_ssem.at[side], s_rsem.at[side],
                to_up if side == 1 else to_down,
            ).start()
        return carry

    lax.fori_loop(0, GD, send_row, 0)

    def own_row(row, carry):
        tiles = smooth_tiles(a_v, t_ext, cols_ref, row, eye)
        slots = [slots_ref[row, m] for m in range(K)]

        def factor(m, slot):
            return jnp.full((B, B), jnp.where(slots[m] == slot, 1.0, 0.0), F32).astype(BF16)

        lanes = pl.ds(pl.multiple_of(row * B, B), B)
        for slot in range(3 * NCG):
            g, h = slot // NCG, slot % NCG
            tile = slot_tile(tiles, factor, slot)
            p_all[row, g + 1, :, h * B : (h + 1) * B] = tile
            turned = tile.T
            for quarter in range(4):
                a, c = quarter // 2, quarter % 2
                first = c * 96 + g * 32
                p_t[2 * h + a, first : first + 32, lanes] = turned[quarter * 32 : quarter * 32 + 32]
        return carry

    lax.fori_loop(0, TR, own_row, 0)

    pc_up.wait_recv()
    pc_down.wait_recv()
    s_up = remote(s_send.at[1], s_halo.at[pl.ds(0, GD)], s_ssem.at[1], s_rsem.at[1], to_up)
    s_down = remote(s_send.at[0], s_halo.at[pl.ds(GD, GD)], s_ssem.at[0], s_rsem.at[0], to_down)
    s_up.wait_recv()
    s_down.wait_recv()

    def halo_rows(region):
        def body(j, carry):
            tiles = [s_halo[region * GD + j, m] for m in range(K)]
            lines = [pc_halo[region, m, pl.ds(j, 1), :] for m in range(K)]

            def factor(m, slot):
                ones = jnp.where(lines[m] == slot, 1.0, 0.0)
                block = jnp.broadcast_to(ones, (16, B)).astype(BF16)
                return jnp.concatenate([block] * (B // 16), axis=0)

            for slot in range(3 * NCG):
                g, h = slot // NCG, slot % NCG
                p_all[TR + region * GD + j, g + 2 * region, :, h * B : (h + 1) * B] = slot_tile(
                    tiles, factor, slot
                )
            return carry

        return body

    for region in range(2):
        lax.fori_loop(0, GD, halo_rows(region), 0)

    def place_row(row, carry):
        cols = [cols_ref[row, k] for k in range(K)]
        left = jnp.concatenate([a_v[row, k] for k in range(K)], axis=1)
        rows = pl.ds(pl.multiple_of(row * B, B), B)
        for g in range(5):
            first = 0 if 1 <= g <= 3 else 1
            right = jnp.concatenate([p_all[cols[k], g] for k in range(first, K)], axis=0)
            value = jnp.dot(left[:, first * B :], right, preferred_element_type=F32)
            ap[g, rows, :] = value.astype(BF16)
        return carry

    lax.fori_loop(0, TR, place_row, 0)

    def block_product(step, target):
        def body(n, carry):
            value = jnp.dot(p_t[target], ap[n], preferred_element_type=F32)
            lanes = pl.ds(pl.multiple_of(n * G, G), G)
            part[step, 0, :, lanes] = value[:96]
            part[step, 1, :, lanes] = value[96:]
            return carry

        lax.fori_loop(0, 5, body, 0)

    HALF = 48
    core_copies, x_copies = [], []
    targets = (xo, xa, xb, x)

    def core_sum(step):
        core_copies[step].wait_recv()
        q[step] = part[step, core] + core_in[step]

    def x_send(src, index, device):
        copy = remote(src, x_in.at[index], x_ssem.at[index], x_rsem.at[index], device)
        copy.start()
        x_copies.append(copy)

    def x_wait(index):
        x_copies[index].wait_recv()

    def finish(step):
        core_sum(step)
        if step == 0:
            x_send(q.at[0, pl.ds(0, HALF)], 0, to_a)
            x_send(q.at[0, pl.ds(HALF, HALF)], 1, to_b)
        elif step == 1:
            x_send(q.at[1, pl.ds(0, HALF)], 2, to_a)
            x_wait(1)
            x_fwd[1] = q[1, HALF:, :] + x_in[1]
        elif step == 2:
            x_send(q.at[2, pl.ds(HALF, HALF)], 3, to_b)
            x_wait(0)
            x_fwd[0] = q[2, :HALF, :] + x_in[0]
            x_send(x_fwd.at[1], 4, to_a)
            x_send(x_fwd.at[0], 5, to_b)

    for step in range(4):
        block_product(step, targets[step])
        copy = remote(
            part.at[step, 1 - core], core_in.at[step], c_ssem.at[step], c_rsem.at[step], to_core
        )
        copy.start()
        core_copies.append(copy)
        if step >= 1:
            finish(step - 1)
    core_sum(3)
    x_wait(2)
    x_wait(5)
    q[3, :HALF, :] = q[3, :HALF, :] + (x_in[2] + x_in[5])
    y_down = remote(q.at[3, pl.ds(0, 32)], y_in.at[1], y_ssem.at[1], y_rsem.at[1], to_down)
    y_down.start()
    x_wait(3)
    x_wait(4)
    q[3, HALF:, :] = q[3, HALF:, :] + (x_in[3] + x_in[4])
    y_up = remote(q.at[3, pl.ds(64, 32)], y_in.at[0], y_ssem.at[0], y_rsem.at[0], to_up)
    y_up.start()
    out_ref[:, :G] = jnp.zeros((32, G), F32)
    out_ref[:, G : 6 * G] = q[3, 32:64, :]
    out_ref[:, 6 * G :] = jnp.zeros((32, G), F32)
    y_up.wait_recv()
    y_down.wait_recv()

    @pl.when(dom > 0)
    def _():
        out_ref[:, : 5 * G] = out_ref[:, : 5 * G] + y_in[0]

    @pl.when(dom < n_dom - 1)
    def _():
        out_ref[:, 2 * G :] = out_ref[:, 2 * G :] + y_in[1]

    for copy in [t_up, t_down, pc_up, pc_down, s_up, s_down, y_up, y_down] + core_copies + x_copies:
        copy.wait_send()


def on_device(a_vals, a_cols, send_rows, tentative, p_cols, ap_cols):
    hbm = pl.BlockSpec(memory_space=pl.ANY)
    smem = pl.BlockSpec(memory_space=pltpu.SMEM)
    dma = pltpu.SemaphoreType.DMA
    return pl.pallas_call(
        kernel,
        out_shape=jax.ShapeDtypeStruct((32, 7 * G), F32),
        in_specs=[hbm, smem, smem, hbm, smem],
        out_specs=pl.BlockSpec(memory_space=pltpu.VMEM),
        scratch_shapes=[
            pltpu.VMEM((TR, K, B, B), BF16),
            pltpu.VMEM((TR, B, B), BF16),
            pltpu.VMEM((TR + 2 * GD, B, B), BF16),
            pltpu.VMEM((2, GD, B, B), BF16),
            pltpu.VMEM((2, GD, K, B, B), BF16),
            pltpu.VMEM((2 * GD, K, B, B), BF16),
            pltpu.VMEM((2, K, GD, B), jnp.int32),
            pltpu.VMEM((2, K, GD, B), jnp.int32),
            pltpu.VMEM((TR + 2 * GD, 5, B, G), BF16),
            pltpu.VMEM((4, 192, TR * B), BF16),
            pltpu.VMEM((5, TR * B, G), BF16),
            pltpu.VMEM((4, 2, 96, 5 * G), F32),
            pltpu.VMEM((4, 96, 5 * G), F32),
            pltpu.VMEM((4, 96, 5 * G), F32),
            pltpu.VMEM((6, 48, 5 * G), F32),
            pltpu.VMEM((2, 48, 5 * G), F32),
            pltpu.VMEM((2, 32, 5 * G), F32),
            dma((3,)),
            dma((2,)), dma((2,)), dma((2,)), dma((2,)), dma((2,)), dma((2,)),
            dma((4,)), dma((4,)), dma((6,)), dma((6,)), dma((2,)), dma((2,)),
        ],
        compiler_params=pltpu.CompilerParams(
            collective_id=0, has_side_effects=True, vmem_limit_bytes=60 * 1024 * 1024
        ),
        cost_estimate=pl.CostEstimate(flops=16_000_000_000, bytes_accessed=8_000_000, transcendentals=0),
    )(a_vals, a_cols, send_rows.reshape(2, GD), tentative, p_cols)


def solution(mesh):
    placed = (
        P(("dom", "sub"), None, None, None),
        P(("dom", "sub"), None),
        P(("dom", "sub"), None, None),
        P(("dom", "sub"), None, None),
        P(("dom", "sub"), None),
        P(("dom", "sub"), None, None),
    )
    return jax.shard_map(
        on_device, mesh=mesh, in_specs=placed, out_specs=P(("dom", "sub"), None), check_vma=False
    )
```

```python
import jax
import jax.numpy as jnp
from jax import lax
from jax.experimental import pallas as pl
from jax.experimental.pallas import tpu as pltpu
from jax.sharding import PartitionSpec as P

B = 128
K = 4
TR = 32
NCG = 2
GD = 8
G = NCG * B
HALF = 48
OMEGA = 0.6
F32 = jnp.float32
BF16 = jnp.bfloat16
MESH = pl.DeviceIdType.MESH


def row_weight(a_v, row, eye):
    diagonal = jnp.sum(jnp.where(eye, a_v[row, 0].astype(F32), 0.0), axis=1, keepdims=True)
    return OMEGA * (1.0 / diagonal)


def smooth_tiles(a_v, t_ext, cols_ref, row, eye, first):
    weight = row_weight(a_v, row, eye)
    tiles = []
    for m in range(first, K):
        product = jnp.dot(a_v[row, m], t_ext[cols_ref[m, row]], preferred_element_type=F32)
        value = weight * product
        value = t_ext[row].astype(F32) - value if m == 0 else -value
        tiles.append(value.astype(BF16))
    return tiles


def slot_tile(tiles, factor, slot):
    total = None
    for m in range(K):
        if m == 0 and slot // NCG != 1:
            continue
        term = tiles[m] * factor(m, slot)
        total = term if total is None else total + term
    return total


def kernel(
    a_hbm, cols_ref, lists_ref, t_hbm, slots_ref, out_ref,
    a_v, t_own, t_ext, t_send, s0_send, s0_halo, s_send, s_halo, pc_send, pc_halo,
    p_all, p_t, ap, part, core_in, q, x1_in, x2_out, x2_in, fin, y_in,
    load_sem, t_ssem, t_rsem, s0_ssem, s0_rsem, s_ssem, s_rsem, pc_ssem, pc_rsem,
    c_ssem, c_rsem, x1_ssem, x1_rsem, x2_ssem, x2_rsem, y_ssem, y_rsem,
):
    dom, sub = lax.axis_index("dom"), lax.axis_index("sub")
    n_dom = lax.axis_size("dom")
    up, down = lax.rem(dom + 1, n_dom), lax.rem(dom + n_dom - 1, n_dom)
    x, core = sub // 2, lax.rem(sub, 2)
    xa = x + 1 - 2 * lax.rem(x, 2)
    xb = 3 - x
    xo = lax.rem(x + 2, 4)
    to_up, to_down = (up, sub), (down, sub)
    to_core = (dom, 2 * x + 1 - core)
    to_a, to_b = (dom, 2 * xa + core), (dom, 2 * xb + core)

    load_own = pltpu.make_async_copy(t_hbm, t_own, load_sem.at[0])
    load_ext = pltpu.make_async_copy(t_hbm, t_ext.at[pl.ds(0, TR)], load_sem.at[1])
    load_a = pltpu.make_async_copy(a_hbm, a_v, load_sem.at[2])
    load_own.start()
    load_a.start()
    load_ext.start()

    barrier = pltpu.get_barrier_semaphore()
    for device in (to_up, to_down, to_core, to_a, to_b):
        pl.semaphore_signal(barrier, inc=1, device_id=device, device_id_type=MESH)

    def remote(src, dst, ssem, rsem, device):
        return pltpu.make_async_remote_copy(
            src_ref=src, dst_ref=dst, send_sem=ssem, recv_sem=rsem,
            device_id=device, device_id_type=MESH,
        )

    eye = lax.broadcasted_iota(jnp.int32, (B, B), 0) == lax.broadcasted_iota(jnp.int32, (B, B), 1)

    load_own.wait()

    def gather_row(j, carry):
        for side in range(2):
            t_send[side, j] = t_own[lists_ref[side, j]]
        return carry

    lax.fori_loop(0, GD, gather_row, 0, unroll=4)

    for side in range(2):
        for j in range(GD):
            row = lists_ref[side, j]
            for m in range(K):
                pc_send[side, m, j : j + 1, :] = jnp.full((1, B), slots_ref[m, row], jnp.int32)

    load_a.wait()

    def first_tile(j, carry):
        for side in range(2):
            row = lists_ref[side, j]
            product = jnp.dot(a_v[row, 0], t_own[row], preferred_element_type=F32)
            value = t_own[row].astype(F32) - row_weight(a_v, row, eye) * product
            s0_send[side, j] = value.astype(BF16)
        return carry

    lax.fori_loop(0, GD, first_tile, 0, unroll=4)
    pl.semaphore_wait(barrier, 5)

    early = []
    for send, halo, ssem, rsem in (
        (t_send, None, t_ssem, t_rsem), (pc_send, pc_halo, pc_ssem, pc_rsem), (s0_send, s0_halo, s0_ssem, s0_rsem),
    ):
        for region, device in ((0, to_up), (1, to_down)):
            target = t_ext.at[pl.ds(TR + GD * region, GD)] if halo is None else halo.at[region]
            early.append(remote(send.at[1 - region], target, ssem.at[region], rsem.at[region], device))
            early[-1].start()

    empty = jnp.zeros((B, G), BF16)

    def clear(first, groups):
        def body(j, carry):
            for g in groups:
                p_all[first + j, g] = empty
            return carry

        return body

    lax.fori_loop(0, TR, clear(0, (0, 4)), 0)
    lax.fori_loop(0, GD, clear(TR, (3, 4)), 0)
    lax.fori_loop(0, GD, clear(TR + GD, (0, 1)), 0)

    load_ext.wait()
    early[0].wait_recv()
    early[1].wait_recv()

    def send_row(j, carry):
        for side in range(2):
            tiles = smooth_tiles(a_v, t_ext, cols_ref, lists_ref[side, j], eye, 1)
            for m in range(1, K):
                s_send[side, j, m - 1] = tiles[m - 1]
            remote(
                s_send.at[side, j], s_halo.at[1 - side, j], s_ssem.at[side], s_rsem.at[side],
                to_up if side == 1 else to_down,
            ).start()
        return carry

    lax.fori_loop(0, GD, send_row, 0, unroll=2)

    def order(target, one, two):
        return jnp.where(target == xo, 0, jnp.where(target == one, 1, jnp.where(target == two, 2, 3)))

    place_of = [[order(t, xa, xb) for t in range(4)], [order(t, xb, xa) for t in range(4)]]

    def own_row(row, carry):
        tiles = smooth_tiles(a_v, t_ext, cols_ref, row, eye, 0)
        slots = [slots_ref[m, row] for m in range(K)]

        def factor(m, slot):
            return jnp.full((B, B), jnp.where(slots[m] == slot, 1.0, 0.0), F32).astype(BF16)

        lanes = pl.ds(pl.multiple_of(row * B, B), B)
        for slot in range(3 * NCG):
            g, h = slot // NCG, slot % NCG
            tile = slot_tile(tiles, factor, slot)
            p_all[row, g + 1, :, h * B : (h + 1) * B] = tile
            turned = tile.T
            for quarter in range(4):
                target, c = 2 * h + quarter // 2, quarter % 2
                for piece in range(2):
                    at = g * 32 + piece * 16
                    first = quarter * 32 + piece * 16
                    half, at = at // HALF, at % HALF
                    p_t[c, half, place_of[half][target], at : at + 16, lanes] = turned[first : first + 16]
        return carry

    lax.fori_loop(0, TR, own_row, 0, unroll=4)

    for copy in early[2:]:
        copy.wait_recv()
    s_up = remote(s_send.at[1], s_halo.at[0], s_ssem.at[1], s_rsem.at[1], to_up)
    s_down = remote(s_send.at[0], s_halo.at[1], s_ssem.at[0], s_rsem.at[0], to_down)
    s_up.wait_recv()
    s_down.wait_recv()

    def halo_rows(j, carry):
        for region in range(2):
            tiles = [s0_halo[region, j]] + [s_halo[region, j, m] for m in range(K - 1)]
            lines = [pc_halo[region, m, pl.ds(j, 1), :] for m in range(K)]

            def factor(m, slot):
                ones = jnp.where(lines[m] == slot, 1.0, 0.0)
                block = jnp.broadcast_to(ones, (16, B)).astype(BF16)
                return jnp.concatenate([block] * (B // 16), axis=0)

            for slot in range(3 * NCG):
                g, h = slot // NCG, slot % NCG
                p_all[TR + region * GD + j, g + 2 * region, :, h * B : (h + 1) * B] = slot_tile(
                    tiles, factor, slot
                )
        return carry

    lax.fori_loop(0, GD, halo_rows, 0)

    def place_group(g):
        first = 0 if 1 <= g <= 3 else 1

        def place_row(row, carry):
            left = jnp.concatenate([a_v[row, k] for k in range(first, K)], axis=1)
            right = jnp.concatenate([p_all[cols_ref[k, row], g] for k in range(first, K)], axis=0)
            value = jnp.dot(left, right, preferred_element_type=F32)
            ap[g, pl.ds(pl.multiple_of(row * B, B), B), :] = value.astype(BF16)
            return carry

        lax.fori_loop(0, TR, place_row, 0, unroll=8)

    core_copies, x1_copies, x2_copies, y_copies = [], [], [], []

    def begin(copies, *args):
        copies.append(remote(*args))
        copies[-1].start()

    def product(n, c):
        left = p_t[c].reshape(8 * HALF, TR * B)
        value = jnp.dot(left, ap[n], preferred_element_type=F32)
        part[n, c] = value.reshape(2, 4, HALF, G)

    def core_stage(n):
        core_copies[n].wait_recv()
        q[n] = part[n, core] + core_in[n]
        for half, device in ((0, to_a), (1, to_b)):
            i = 2 * n + half
            begin(
                x1_copies, q.at[n, half, pl.ds(0, 2)], x1_in.at[n, half],
                x1_ssem.at[i], x1_rsem.at[i], device,
            )

    def x1_stage(n):
        for half, device in ((0, to_b), (1, to_a)):
            i = 2 * n + half
            x1_copies[i].wait_recv()
            x2_out[n, half] = q[n, half, 2] + x1_in[n, half, 0]
            begin(
                x2_copies, x2_out.at[n, half], x2_in.at[n, half],
                x2_ssem.at[i], x2_rsem.at[i], device,
            )

    def x2_stage(n):
        for half in range(2):
            x2_copies[2 * n + half].wait_recv()
            fin[n, half * HALF : (half + 1) * HALF] = q[n, half, 3] + x1_in[n, half, 1] + x2_in[n, half]
        for region, device in ((0, to_up), (1, to_down)):
            i = 2 * n + region
            begin(
                y_copies, fin.at[n, pl.ds(64 - 64 * region, 32)], y_in.at[n, region],
                y_ssem.at[i], y_rsem.at[i], device,
            )

    for n in range(5):
        place_group(n)
        if n >= 1:
            core_stage(n - 1)
        if n >= 2:
            x1_stage(n - 2)
        if n >= 3:
            x2_stage(n - 3)
        product(n, 1 - core)
        begin(core_copies, part.at[n, 1 - core], core_in.at[n], c_ssem.at[n], c_rsem.at[n], to_core)
        product(n, core)
    core_stage(4)
    x1_stage(3)
    x2_stage(2)
    x1_stage(4)
    x2_stage(3)
    x2_stage(4)
    for copy in y_copies:
        copy.wait_recv()
    for g in range(7):
        total = None
        for n, value in (
            (g - 1, lambda n: fin[n, 32:64]),
            (g, lambda n: jnp.where(dom > 0, y_in[n, 0], 0.0)),
            (g - 2, lambda n: jnp.where(dom < n_dom - 1, y_in[n, 1], 0.0)),
        ):
            if 0 <= n < 5:
                total = value(n) if total is None else total + value(n)
        out_ref[:, g * G : (g + 1) * G] = total

    for copy in early + [s_up, s_down] + core_copies + x1_copies + x2_copies + y_copies:
        copy.wait_send()


def on_device(a_vals, a_cols, send_rows, tentative, p_cols, ap_cols):
    hbm = pl.BlockSpec(memory_space=pl.ANY)
    smem = pl.BlockSpec(memory_space=pltpu.SMEM)
    dma = pltpu.SemaphoreType.DMA
    return pl.pallas_call(
        kernel,
        out_shape=jax.ShapeDtypeStruct((32, 7 * G), F32),
        in_specs=[hbm, smem, smem, hbm, smem],
        out_specs=pl.BlockSpec(memory_space=pltpu.VMEM),
        scratch_shapes=[
            pltpu.VMEM((TR, K, B, B), BF16),
            pltpu.VMEM((TR, B, B), BF16),
            pltpu.VMEM((TR + 2 * GD, B, B), BF16),
            pltpu.VMEM((2, GD, B, B), BF16),
            pltpu.VMEM((2, GD, B, B), BF16),
            pltpu.VMEM((2, GD, B, B), BF16),
            pltpu.VMEM((2, GD, K - 1, B, B), BF16),
            pltpu.VMEM((2, GD, K - 1, B, B), BF16),
            pltpu.VMEM((2, K, GD, B), jnp.int32),
            pltpu.VMEM((2, K, GD, B), jnp.int32),
            pltpu.VMEM((TR + 2 * GD, 5, B, G), BF16),
            pltpu.VMEM((2, 2, 4, HALF, TR * B), BF16),
            pltpu.VMEM((5, TR * B, G), BF16),
            pltpu.VMEM((5, 2, 2, 4, HALF, G), F32),
            pltpu.VMEM((5, 2, 4, HALF, G), F32),
            pltpu.VMEM((5, 2, 4, HALF, G), F32),
            pltpu.VMEM((5, 2, 2, HALF, G), F32),
            pltpu.VMEM((5, 2, HALF, G), F32),
            pltpu.VMEM((5, 2, HALF, G), F32),
            pltpu.VMEM((5, 2 * HALF, G), F32),
            pltpu.VMEM((5, 2, 32, G), F32),
            dma((3,)),
            dma((2,)), dma((2,)), dma((2,)), dma((2,)), dma((2,)), dma((2,)), dma((2,)), dma((2,)),
            dma((5,)), dma((5,)), dma((10,)), dma((10,)), dma((10,)), dma((10,)), dma((10,)), dma((10,)),
        ],
        compiler_params=pltpu.CompilerParams(
            collective_id=0, has_side_effects=True, vmem_limit_bytes=60 * 1024 * 1024
        ),
        cost_estimate=pl.CostEstimate(flops=16_000_000_000, bytes_accessed=8_000_000, transcendentals=0),
    )(a_vals, a_cols.T, send_rows.reshape(2, GD), tentative, p_cols.T)


def solution(mesh):
    placed = (
        P(("dom", "sub"), None, None, None),
        P(("dom", "sub"), None),
        P(("dom", "sub"), None, None),
        P(("dom", "sub"), None, None),
        P(("dom", "sub"), None),
        P(("dom", "sub"), None, None),
    )
    return jax.shard_map(
        on_device, mesh=mesh, in_specs=placed, out_specs=P(("dom", "sub"), None), check_vma=False
    )
```

```python
import jax
import jax.numpy as jnp
from jax import lax
from jax.experimental import pallas as pl
from jax.experimental.pallas import tpu as pltpu
from jax.sharding import PartitionSpec as P

B = 128
K = 4
TR = 32
NCG = 2
GD = 8
G = NCG * B
HB = B // 2
R3 = 96
OMEGA = 0.6
F32 = jnp.float32
BF16 = jnp.bfloat16
MESH = pl.DeviceIdType.MESH


def row_weight(a_v, row, eye):
    diagonal = jnp.sum(jnp.where(eye, a_v[row, 0].astype(F32), 0.0), axis=1, keepdims=True)
    return OMEGA * (1.0 / diagonal)


def smooth_tiles(a_v, t_ext, cols_ref, row, eye, first):
    weight = row_weight(a_v, row, eye)
    tiles = []
    for m in range(first, K):
        product = jnp.dot(a_v[row, m], t_ext[cols_ref[m, row]], preferred_element_type=F32)
        value = weight * product
        value = t_ext[row].astype(F32) - value if m == 0 else -value
        tiles.append(value.astype(BF16))
    return tiles


def doubled(tile, half):
    part = tile[:, half * HB : (half + 1) * HB]
    return jnp.concatenate([part, part], axis=1)


def paired(one, two, half):
    columns = slice(half * HB, (half + 1) * HB)
    return jnp.concatenate([one[:, columns], two[:, columns]], axis=1)


def group_tile(doubles, slots, group):
    wanted = NCG * group + (lax.broadcasted_iota(jnp.int32, (1, B), 1) >= HB).astype(jnp.int32)
    total = None
    for m in range(K):
        if m == 0 and group != 1:
            continue
        ones = jnp.where(slots[m] == wanted, 1.0, 0.0)
        block = jnp.broadcast_to(ones, (16, B)).astype(BF16)
        term = doubles[m] * jnp.concatenate([block] * (B // 16), axis=0)
        total = term if total is None else total + term
    return total


def chunk_of(half, group):
    return (4, half) if group == 4 else (2 * half + group // 2, group % 2)


def put(p_all, row, half, group, tile):
    chunk, at = chunk_of(half, group)
    p_all[row, chunk, :, at * B : (at + 1) * B] = tile


def clear_rows(p_all):
    empty = jnp.zeros((B, B), BF16)
    for first, count, groups in ((0, TR, (0, 4)), (TR, GD, (3, 4)), (TR + GD, GD, (0, 1))):

        def body(j, carry, first=first, groups=groups):
            for group in groups:
                for half in range(2):
                    put(p_all, first + j, half, group, empty)
            return carry

        lax.fori_loop(0, count, body, 0, unroll=2)


def identity_mask():
    return lax.broadcasted_iota(jnp.int32, (B, B), 0) == lax.broadcasted_iota(jnp.int32, (B, B), 1)


def first_tiles(a_v, t_own, lists_ref, s0_send):
    eye = identity_mask()

    def body(j, carry):
        for side in range(2):
            row = lists_ref[side, j]
            product = jnp.dot(a_v[row, 0], t_own[row], preferred_element_type=F32)
            value = t_own[row].astype(F32) - row_weight(a_v, row, eye) * product
            s0_send[side, j] = value.astype(BF16)
        return carry

    lax.fori_loop(0, GD, body, 0, unroll=4)


def send_rows(a_v, t_ext, cols_ref, lists_ref, s_send, start):
    eye = identity_mask()

    def body(pair, carry):
        for side in range(2):
            one, two = (
                smooth_tiles(a_v, t_ext, cols_ref, lists_ref[side, 2 * pair + e], eye, 1) for e in range(2)
            )
            for half in range(2):
                s_send[half, side, pair, 0] = paired(one[0], one[1], half)
                s_send[half, side, pair, 1] = paired(two[0], two[1], half)
                s_send[half, side, pair, 2] = paired(one[2], two[2], half)
            start(side, pair)
        return carry

    lax.fori_loop(0, GD // 2, body, 0, unroll=2)


def own_rows(a_v, t_ext, cols_ref, slots_ref, p_all, p_t, place_of):
    eye = identity_mask()

    def body(row, carry):
        tiles = smooth_tiles(a_v, t_ext, cols_ref, row, eye, 0)
        slots = [slots_ref[m, row] for m in range(K)]
        lanes = pl.ds(pl.multiple_of(row * B, B), B)
        for half in range(2):
            doubles = [doubled(tile, half) for tile in tiles]
            for group in range(3):
                tile = group_tile(doubles, slots, group)
                put(p_all, row, half, group + 1, tile)
                turned = tile.T
                for s in range(2):
                    for c in range(2):
                        first = s * HB + c * 32
                        p_t[c, place_of[2 * s + half], group * 32 : group * 32 + 32, lanes] = turned[
                            first : first + 32
                        ]
        return carry

    lax.fori_loop(0, TR, body, 0, unroll=4)


def halo_rows(half, s0_halo, s_halo, pc_halo, p_all):
    def body(pair, carry):
        for region in range(2):
            for e in range(2):
                j = 2 * pair + e
                both, third = s_halo[half, region, pair, e], s_halo[half, region, pair, 2]
                doubles = [
                    doubled(s0_halo[region, j], half), doubled(both, 0), doubled(both, 1), doubled(third, e),
                ]
                slots = [pc_halo[region, m, pl.ds(j, 1), :] for m in range(K)]
                for group in range(3):
                    put(
                        p_all, TR + region * GD + j, half, group + 2 * region,
                        group_tile(doubles, slots, group),
                    )
        return carry

    lax.fori_loop(0, GD // 2, body, 0)


def place_chunk(n, a_v, cols_ref, p_all, ap):
    first = 1 if n == 4 else 0

    def body(row, carry):
        left = jnp.concatenate([a_v[row, k] for k in range(first, K)], axis=1)
        right = jnp.concatenate([p_all[cols_ref[k, row], n] for k in range(first, K)], axis=0)
        value = jnp.dot(left, right, preferred_element_type=F32)
        ap[n, pl.ds(pl.multiple_of(row * B, B), B), :] = value.astype(BF16)
        return carry

    lax.fori_loop(0, TR, body, 0, unroll=16)


def product_chunk(n, c, p_t, ap, part):
    left = p_t[c].reshape(4 * R3, TR * B)
    value = jnp.dot(left, ap[n], preferred_element_type=F32)
    part[n, c] = value.reshape(4, R3, G)


def kernel(
    a_hbm, cols_ref, lists_ref, t_hbm, slots_ref, out_ref,
    a_v, t_own, t_ext, t_send, s0_send, s0_halo, s_send, s_halo, pc_send, pc_halo,
    p_all, p_t, ap, part, core_in, q, x_in, fin, y_in,
    load_sem, t_ssem, t_rsem, s0_ssem, s0_rsem, s_ssem, s_rsem, pc_ssem, pc_rsem,
    c_ssem, c_rsem, x_ssem, x_rsem, y_ssem, y_rsem,
):
    dom, sub = lax.axis_index("dom"), lax.axis_index("sub")
    n_dom = lax.axis_size("dom")
    up, down = lax.rem(dom + 1, n_dom), lax.rem(dom + n_dom - 1, n_dom)
    x, core = sub // 2, lax.rem(sub, 2)
    xa = x + 1 - 2 * lax.rem(x, 2)
    xb = 3 - x
    xo = lax.rem(x + 2, 4)
    to_up, to_down = (up, sub), (down, sub)
    to_core = (dom, 2 * x + 1 - core)
    to_ring = tuple((dom, 2 * chip + core) for chip in (xa, xb, xo))

    load_own = pltpu.make_async_copy(t_hbm, t_own, load_sem.at[0])
    load_ext = pltpu.make_async_copy(t_hbm, t_ext.at[pl.ds(0, TR)], load_sem.at[1])
    load_a = pltpu.make_async_copy(a_hbm, a_v, load_sem.at[2])
    load_own.start()
    load_a.start()
    load_ext.start()

    barrier = pltpu.get_barrier_semaphore()
    for device in (to_up, to_down, to_core) + to_ring:
        pl.semaphore_signal(barrier, inc=1, device_id=device, device_id_type=MESH)

    def remote(src, dst, ssem, rsem, device):
        return pltpu.make_async_remote_copy(
            src_ref=src, dst_ref=dst, send_sem=ssem, recv_sem=rsem,
            device_id=device, device_id_type=MESH,
        )

    load_own.wait()

    def gather_row(j, carry):
        for side in range(2):
            t_send[side, j] = t_own[lists_ref[side, j]]
        return carry

    lax.fori_loop(0, GD, gather_row, 0, unroll=4)

    for side in range(2):
        for j in range(GD):
            row = lists_ref[side, j]
            for m in range(K):
                pc_send[side, m, j : j + 1, :] = jnp.full((1, B), slots_ref[m, row], jnp.int32)

    load_a.wait()
    first_tiles(a_v, t_own, lists_ref, s0_send)
    pl.semaphore_wait(barrier, 6)

    early = []
    for send, halo, ssem, rsem in (
        (t_send, None, t_ssem, t_rsem), (pc_send, pc_halo, pc_ssem, pc_rsem), (s0_send, s0_halo, s0_ssem, s0_rsem),
    ):
        for region, device in ((0, to_up), (1, to_down)):
            target = t_ext.at[pl.ds(TR + GD * region, GD)] if halo is None else halo.at[region]
            early.append(remote(send.at[1 - region], target, ssem.at[region], rsem.at[region], device))
            early[-1].start()

    clear_rows(p_all)
    load_ext.wait()
    early[0].wait_recv()
    early[1].wait_recv()

    def start_pair(side, pair):
        remote(
            s_send.at[0, side, pair], s_halo.at[0, 1 - side, pair], s_ssem.at[0, side], s_rsem.at[0, side],
            to_up if side == 1 else to_down,
        ).start()

    send_rows(a_v, t_ext, cols_ref, lists_ref, s_send, start_pair)

    def side_copy(half, side):
        return remote(
            s_send.at[half, side], s_halo.at[half, 1 - side], s_ssem.at[half, side], s_rsem.at[half, side],
            to_up if side == 1 else to_down,
        )

    s_copies = [[side_copy(half, side) for side in range(2)] for half in range(2)]

    place_of = [
        jnp.where(t == xa, 0, jnp.where(t == xb, 1, jnp.where(t == xo, 2, 3))) for t in range(4)
    ]
    own_rows(a_v, t_ext, cols_ref, slots_ref, p_all, p_t, place_of)
    for copy in s_copies[1]:
        copy.start()

    core_copies, x_copies, y_copies = [], [], []

    def begin(copies, *args):
        copies.append(remote(*args))
        copies[-1].start()

    def core_stage(n):
        core_copies[n].wait_recv()
        q[n] = part[n, core] + core_in[n]
        for t in range(3):
            i = 3 * n + t
            begin(x_copies, q.at[n, t], x_in.at[n, t], x_ssem.at[i], x_rsem.at[i], to_ring[t])

    def x_stage(n):
        for t in range(3):
            x_copies[3 * n + t].wait_recv()
        fin[n] = (q[n, 3] + x_in[n, 0]) + (x_in[n, 1] + x_in[n, 2])
        for region, device in ((0, to_up), (1, to_down)):
            i = 2 * n + region
            begin(
                y_copies, fin.at[n, pl.ds(64 - 64 * region, 32)], y_in.at[n, region],
                y_ssem.at[i], y_rsem.at[i], device,
            )

    def place(n):
        place_chunk(n, a_v, cols_ref, p_all, ap)

    def product(n):
        product_chunk(n, 1 - core, p_t, ap, part)
        begin(core_copies, part.at[n, 1 - core], core_in.at[n], c_ssem.at[n], c_rsem.at[n], to_core)
        product_chunk(n, core, p_t, ap, part)

    for copy in early[2:] + s_copies[0]:
        copy.wait_recv()
    halo_rows(0, s0_halo, s_halo, pc_halo, p_all)
    place(0)
    product(0)
    place(1)
    core_stage(0)
    product(1)
    for copy in s_copies[1]:
        copy.wait_recv()
    halo_rows(1, s0_halo, s_halo, pc_halo, p_all)
    place(2)
    core_stage(1)
    product(2)
    place(3)
    core_stage(2)
    product(3)
    place(4)
    core_stage(3)
    x_stage(0)
    product(4)
    x_stage(1)
    core_stage(4)
    x_stage(2)
    x_stage(3)
    x_stage(4)
    for copy in y_copies:
        copy.wait_recv()

    def columns(array, half, group):
        chunk, at = chunk_of(half, group)
        return array(chunk)[:, at * B : (at + 1) * B]

    for g in range(7):
        halves = []
        for half in range(2):
            total = None
            for group, array in (
                (g - 1, lambda n: fin[n, 32:64]),
                (g, lambda n: jnp.where(dom > 0, y_in[n, 0], 0.0)),
                (g - 2, lambda n: jnp.where(dom < n_dom - 1, y_in[n, 1], 0.0)),
            ):
                if 0 <= group < 5:
                    value = columns(array, half, group)
                    total = value if total is None else total + value
            halves.append(total)
        for s in range(2):
            out_ref[:, g * G + s * B : g * G + (s + 1) * B] = paired(halves[0], halves[1], s)

    for copy in early + s_copies[0] + s_copies[1] + core_copies + x_copies + y_copies:
        copy.wait_send()


def on_device(a_vals, a_cols, send_rows, tentative, p_cols, ap_cols):
    hbm = pl.BlockSpec(memory_space=pl.ANY)
    smem = pl.BlockSpec(memory_space=pltpu.SMEM)
    dma = pltpu.SemaphoreType.DMA
    return pl.pallas_call(
        kernel,
        out_shape=jax.ShapeDtypeStruct((32, 7 * G), F32),
        in_specs=[hbm, smem, smem, hbm, smem],
        out_specs=pl.BlockSpec(memory_space=pltpu.VMEM),
        scratch_shapes=[
            pltpu.VMEM((TR, K, B, B), BF16),
            pltpu.VMEM((TR, B, B), BF16),
            pltpu.VMEM((TR + 2 * GD, B, B), BF16),
            pltpu.VMEM((2, GD, B, B), BF16),
            pltpu.VMEM((2, GD, B, B), BF16),
            pltpu.VMEM((2, GD, B, B), BF16),
            pltpu.VMEM((2, 2, GD // 2, K - 1, B, B), BF16),
            pltpu.VMEM((2, 2, GD // 2, K - 1, B, B), BF16),
            pltpu.VMEM((2, K, GD, B), jnp.int32),
            pltpu.VMEM((2, K, GD, B), jnp.int32),
            pltpu.VMEM((TR + 2 * GD, 5, B, G), BF16),
            pltpu.VMEM((2, 4, R3, TR * B), BF16),
            pltpu.VMEM((5, TR * B, G), BF16),
            pltpu.VMEM((5, 2, 4, R3, G), F32),
            pltpu.VMEM((5, 4, R3, G), F32),
            pltpu.VMEM((5, 4, R3, G), F32),
            pltpu.VMEM((5, 3, R3, G), F32),
            pltpu.VMEM((5, R3, G), F32),
            pltpu.VMEM((5, 2, 32, G), F32),
            dma((3,)),
            dma((2,)), dma((2,)), dma((2,)), dma((2,)), dma((2, 2)), dma((2, 2)), dma((2,)), dma((2,)),
            dma((5,)), dma((5,)), dma((15,)), dma((15,)), dma((10,)), dma((10,)),
        ],
        compiler_params=pltpu.CompilerParams(
            collective_id=0, has_side_effects=True, vmem_limit_bytes=60 * 1024 * 1024
        ),
        cost_estimate=pl.CostEstimate(flops=16_000_000_000, bytes_accessed=8_000_000, transcendentals=0),
    )(a_vals, a_cols.T, send_rows.reshape(2, GD), tentative, p_cols.T)


def solution(mesh):
    placed = (
        P(("dom", "sub"), None, None, None),
        P(("dom", "sub"), None),
        P(("dom", "sub"), None, None),
        P(("dom", "sub"), None, None),
        P(("dom", "sub"), None),
        P(("dom", "sub"), None, None),
    )
    return jax.shard_map(
        on_device, mesh=mesh, in_specs=placed, out_specs=P(("dom", "sub"), None), check_vma=False
    )
```

```python
import jax
import jax.numpy as jnp
from jax import lax
from jax.experimental import pallas as pl
from jax.experimental.pallas import tpu as pltpu
from jax.sharding import PartitionSpec as P

B = 128
K = 4
TR = 32
NCG = 2
GD = 8
G = NCG * B
HB = B // 2
R3 = 96
OMEGA = 0.6
F32 = jnp.float32
BF16 = jnp.bfloat16
MESH = pl.DeviceIdType.MESH


def row_weight(a_v, row, eye):
    diagonal = jnp.sum(jnp.where(eye, a_v[row, 0].astype(F32), 0.0), axis=1, keepdims=True)
    return OMEGA * (1.0 / diagonal)


def smooth_tiles(a_v, t_ext, cols_ref, row, eye, first):
    weight = row_weight(a_v, row, eye)
    tiles = []
    for m in range(first, K):
        product = jnp.dot(a_v[row, m], t_ext[cols_ref[m, row]], preferred_element_type=F32)
        value = weight * product
        value = t_ext[row].astype(F32) - value if m == 0 else -value
        tiles.append(value.astype(BF16))
    return tiles


def doubled(tile, half):
    part = tile[:, half * HB : (half + 1) * HB]
    return jnp.concatenate([part, part], axis=1)


def paired(one, two, half):
    columns = slice(half * HB, (half + 1) * HB)
    return jnp.concatenate([one[:, columns], two[:, columns]], axis=1)


def group_tile(doubles, slots, group):
    wanted = NCG * group + (lax.broadcasted_iota(jnp.int32, (1, B), 1) >= HB).astype(jnp.int32)
    total = None
    for m in range(K):
        if m == 0 and group != 1:
            continue
        ones = jnp.where(slots[m] == wanted, 1.0, 0.0)
        block = jnp.broadcast_to(ones, (16, B)).astype(BF16)
        term = doubles[m] * jnp.concatenate([block] * (B // 16), axis=0)
        total = term if total is None else total + term
    return total


def chunk_of(half, group):
    return (4, half) if group == 4 else (2 * half + group // 2, group % 2)


def put(p_all, row, half, group, tile):
    chunk, at = chunk_of(half, group)
    p_all[row, chunk, :, at * B : (at + 1) * B] = tile


def clear_rows(p_all):
    empty = jnp.zeros((B, B), BF16)
    for first, count, groups in ((0, TR, (0, 4)), (TR, GD, (3, 4)), (TR + GD, GD, (0, 1))):

        def body(j, carry, first=first, groups=groups):
            for group in groups:
                for half in range(2):
                    put(p_all, first + j, half, group, empty)
            return carry

        lax.fori_loop(0, count, body, 0, unroll=2)


def identity_mask():
    return lax.broadcasted_iota(jnp.int32, (B, B), 0) == lax.broadcasted_iota(jnp.int32, (B, B), 1)


def first_tiles(a_v, t_own, lists_ref, s0_send):
    eye = identity_mask()

    def body(j, carry):
        for side in range(2):
            row = lists_ref[side, j]
            product = jnp.dot(a_v[row, 0], t_own[row], preferred_element_type=F32)
            value = t_own[row].astype(F32) - row_weight(a_v, row, eye) * product
            s0_send[side, j] = value.astype(BF16)
        return carry

    lax.fori_loop(0, GD, body, 0, unroll=4)


def send_rows(a_v, t_ext, cols_ref, lists_ref, s_send, start):
    eye = identity_mask()

    def body(pair, carry):
        for side in range(2):
            one, two = (
                smooth_tiles(a_v, t_ext, cols_ref, lists_ref[side, 2 * pair + e], eye, 1) for e in range(2)
            )
            for half in range(2):
                s_send[half, side, pair, 0] = paired(one[0], one[1], half)
                s_send[half, side, pair, 1] = paired(two[0], two[1], half)
                s_send[half, side, pair, 2] = paired(one[2], two[2], half)
            start(side, pair)
        return carry

    lax.fori_loop(0, GD // 2, body, 0, unroll=2)


def own_rows(a_v, t_ext, cols_ref, slots_ref, p_all, p_t, place_of):
    eye = identity_mask()

    def body(row, carry):
        tiles = smooth_tiles(a_v, t_ext, cols_ref, row, eye, 0)
        slots = [slots_ref[m, row] for m in range(K)]
        lanes = pl.ds(pl.multiple_of(row * B, B), B)
        for half in range(2):
            doubles = [doubled(tile, half) for tile in tiles]
            for group in range(3):
                tile = group_tile(doubles, slots, group)
                put(p_all, row, half, group + 1, tile)
                turned = tile.T
                for s in range(2):
                    for c in range(2):
                        first = s * HB + c * 32
                        p_t[c, place_of[2 * s + half], group * 32 : group * 32 + 32, lanes] = turned[
                            first : first + 32
                        ]
        return carry

    lax.fori_loop(0, TR, body, 0, unroll=4)


def halo_rows(half, s0_halo, s_halo, pc_halo, p_all):
    def body(pair, carry):
        for region in range(2):
            for e in range(2):
                j = 2 * pair + e
                both, third = s_halo[half, region, pair, e], s_halo[half, region, pair, 2]
                doubles = [
                    doubled(s0_halo[region, j], half), doubled(both, 0), doubled(both, 1), doubled(third, e),
                ]
                slots = [pc_halo[region, m, pl.ds(j, 1), :] for m in range(K)]
                for group in range(3):
                    put(
                        p_all, TR + region * GD + j, half, group + 2 * region,
                        group_tile(doubles, slots, group),
                    )
        return carry

    lax.fori_loop(0, GD // 2, body, 0)


def place_chunk(n, a_v, cols_ref, p_all, ap):
    first = 1 if n == 4 else 0

    def body(row, carry):
        left = jnp.concatenate([a_v[row, k] for k in range(first, K)], axis=1)
        right = jnp.concatenate([p_all[cols_ref[k, row], n] for k in range(first, K)], axis=0)
        value = jnp.dot(left, right, preferred_element_type=F32)
        ap[n, pl.ds(pl.multiple_of(row * B, B), B), :] = value.astype(BF16)
        return carry

    lax.fori_loop(0, TR, body, 0, unroll=16)


def product_chunk(n, c, p_t, ap, part):
    left = p_t[c].reshape(4 * R3, TR * B)
    value = jnp.dot(left, ap[n], preferred_element_type=F32)
    part[n, c] = value.reshape(4, R3, G)


STEPS = 32000.0
LIFT = 10


def encode(block, coded):
    top = jnp.max(jnp.abs(block), axis=0, keepdims=True)
    exponent = jnp.clip(jnp.ceil(jnp.log2(jnp.maximum(top, 1e-37))), -116.0, 128.0)
    scaled = (block * jnp.exp2(LIFT - exponent)) * (STEPS / 2**LIFT)
    coded[:R3] = jnp.round(scaled).astype(jnp.int32).astype(jnp.int16)
    coded[R3:] = jnp.broadcast_to(exponent, (16, G)).astype(jnp.int32).astype(jnp.int16)


def decode(coded):
    exponent = coded[R3:].astype(jnp.int32).astype(F32)[:1]
    values = coded[:R3].astype(jnp.int32).astype(F32)
    return (values * (2**LIFT / STEPS)) * jnp.exp2(exponent - LIFT)


def kernel(
    a_hbm, cols_ref, lists_ref, t_hbm, slots_ref, out_ref,
    a_v, t_own, t_ext, t_send, s0_send, s0_halo, s_send, s_halo, pc_send, pc_halo,
    p_all, p_t, ap, part, core_in, q, x_out, x_in, fin, y_in,
    load_sem, t_ssem, t_rsem, s0_ssem, s0_rsem, s_ssem, s_rsem, pc_ssem, pc_rsem,
    c_ssem, c_rsem, x_ssem, x_rsem, y_ssem, y_rsem,
):
    dom, sub = lax.axis_index("dom"), lax.axis_index("sub")
    n_dom = lax.axis_size("dom")
    up, down = lax.rem(dom + 1, n_dom), lax.rem(dom + n_dom - 1, n_dom)
    x, core = sub // 2, lax.rem(sub, 2)
    xa = x + 1 - 2 * lax.rem(x, 2)
    xb = 3 - x
    xo = lax.rem(x + 2, 4)
    to_up, to_down = (up, sub), (down, sub)
    to_core = (dom, 2 * x + 1 - core)
    to_ring = tuple((dom, 2 * chip + core) for chip in (xa, xb, xo))

    load_own = pltpu.make_async_copy(t_hbm, t_own, load_sem.at[0])
    load_ext = pltpu.make_async_copy(t_hbm, t_ext.at[pl.ds(0, TR)], load_sem.at[1])
    load_a = pltpu.make_async_copy(a_hbm, a_v, load_sem.at[2])
    load_own.start()
    load_a.start()
    load_ext.start()

    barrier = pltpu.get_barrier_semaphore()
    for device in (to_up, to_down, to_core) + to_ring:
        pl.semaphore_signal(barrier, inc=1, device_id=device, device_id_type=MESH)

    def remote(src, dst, ssem, rsem, device):
        return pltpu.make_async_remote_copy(
            src_ref=src, dst_ref=dst, send_sem=ssem, recv_sem=rsem,
            device_id=device, device_id_type=MESH,
        )

    load_own.wait()

    def gather_row(j, carry):
        for side in range(2):
            t_send[side, j] = t_own[lists_ref[side, j]]
        return carry

    lax.fori_loop(0, GD, gather_row, 0, unroll=4)

    for side in range(2):
        for j in range(GD):
            row = lists_ref[side, j]
            for m in range(K):
                pc_send[side, m, j : j + 1, :] = jnp.full((1, B), slots_ref[m, row], jnp.int32)

    load_a.wait()
    first_tiles(a_v, t_own, lists_ref, s0_send)
    pl.semaphore_wait(barrier, 6)

    early = []
    for send, halo, ssem, rsem in (
        (t_send, None, t_ssem, t_rsem), (pc_send, pc_halo, pc_ssem, pc_rsem), (s0_send, s0_halo, s0_ssem, s0_rsem),
    ):
        for region, device in ((0, to_up), (1, to_down)):
            target = t_ext.at[pl.ds(TR + GD * region, GD)] if halo is None else halo.at[region]
            early.append(remote(send.at[1 - region], target, ssem.at[region], rsem.at[region], device))
            early[-1].start()

    clear_rows(p_all)
    load_ext.wait()
    early[0].wait_recv()
    early[1].wait_recv()

    def start_pair(side, pair):
        remote(
            s_send.at[0, side, pair], s_halo.at[0, 1 - side, pair], s_ssem.at[0, side], s_rsem.at[0, side],
            to_up if side == 1 else to_down,
        ).start()

    send_rows(a_v, t_ext, cols_ref, lists_ref, s_send, start_pair)

    def side_copy(half, side):
        return remote(
            s_send.at[half, side], s_halo.at[half, 1 - side], s_ssem.at[half, side], s_rsem.at[half, side],
            to_up if side == 1 else to_down,
        )

    s_copies = [[side_copy(half, side) for side in range(2)] for half in range(2)]

    place_of = [
        jnp.where(t == xa, 0, jnp.where(t == xb, 1, jnp.where(t == xo, 2, 3))) for t in range(4)
    ]
    own_rows(a_v, t_ext, cols_ref, slots_ref, p_all, p_t, place_of)
    for copy in s_copies[1]:
        copy.start()

    core_copies, x_copies, y_copies = [], [None] * 15, []

    def begin(copies, *args):
        copies.append(remote(*args))
        copies[-1].start()

    def core_stage(n):
        core_copies[n].wait_recv()
        for t in (2, 0, 1):
            i = 3 * n + t
            encode(part[n, core, t] + core_in[n, t], x_out.at[n, t])
            x_copies[i] = remote(x_out.at[n, t], x_in.at[n, t], x_ssem.at[i], x_rsem.at[i], to_ring[t])
            x_copies[i].start()
        q[n] = part[n, core, 3] + core_in[n, 3]

    def x_stage(n):
        for t in range(3):
            x_copies[3 * n + t].wait_recv()
        fin[n] = (q[n] + decode(x_in.at[n, 0])) + (decode(x_in.at[n, 1]) + decode(x_in.at[n, 2]))
        for region, device in ((0, to_up), (1, to_down)):
            i = 2 * n + region
            begin(
                y_copies, fin.at[n, pl.ds(64 - 64 * region, 32)], y_in.at[n, region],
                y_ssem.at[i], y_rsem.at[i], device,
            )

    def place(n):
        place_chunk(n, a_v, cols_ref, p_all, ap)

    def product(n):
        for c in range(2):
            product_chunk(n, c, p_t, ap, part)
        begin(core_copies, part.at[n, 1 - core], core_in.at[n], c_ssem.at[n], c_rsem.at[n], to_core)

    for copy in early[2:] + s_copies[0]:
        copy.wait_recv()
    halo_rows(0, s0_halo, s_halo, pc_halo, p_all)
    place(0)
    product(0)
    place(1)
    core_stage(0)
    product(1)
    for copy in s_copies[1]:
        copy.wait_recv()
    halo_rows(1, s0_halo, s_halo, pc_halo, p_all)
    place(2)
    core_stage(1)
    product(2)
    place(3)
    core_stage(2)
    product(3)
    place(4)
    core_stage(3)
    x_stage(0)
    product(4)
    x_stage(1)
    core_stage(4)
    x_stage(2)
    x_stage(3)
    x_stage(4)
    for copy in y_copies:
        copy.wait_recv()

    def columns(array, half, group):
        chunk, at = chunk_of(half, group)
        return array(chunk)[:, at * B : (at + 1) * B]

    for g in range(7):
        halves = []
        for half in range(2):
            total = None
            for group, array in (
                (g - 1, lambda n: fin[n, 32:64]),
                (g, lambda n: jnp.where(dom > 0, y_in[n, 0], 0.0)),
                (g - 2, lambda n: jnp.where(dom < n_dom - 1, y_in[n, 1], 0.0)),
            ):
                if 0 <= group < 5:
                    value = columns(array, half, group)
                    total = value if total is None else total + value
            halves.append(total)
        for s in range(2):
            out_ref[:, g * G + s * B : g * G + (s + 1) * B] = paired(halves[0], halves[1], s)

    for copy in early + s_copies[0] + s_copies[1] + core_copies + x_copies + y_copies:
        copy.wait_send()


def on_device(a_vals, a_cols, send_rows, tentative, p_cols, ap_cols):
    hbm = pl.BlockSpec(memory_space=pl.ANY)
    smem = pl.BlockSpec(memory_space=pltpu.SMEM)
    dma = pltpu.SemaphoreType.DMA
    return pl.pallas_call(
        kernel,
        out_shape=jax.ShapeDtypeStruct((32, 7 * G), F32),
        in_specs=[hbm, smem, smem, hbm, smem],
        out_specs=pl.BlockSpec(memory_space=pltpu.VMEM),
        scratch_shapes=[
            pltpu.VMEM((TR, K, B, B), BF16),
            pltpu.VMEM((TR, B, B), BF16),
            pltpu.VMEM((TR + 2 * GD, B, B), BF16),
            pltpu.VMEM((2, GD, B, B), BF16),
            pltpu.VMEM((2, GD, B, B), BF16),
            pltpu.VMEM((2, GD, B, B), BF16),
            pltpu.VMEM((2, 2, GD // 2, K - 1, B, B), BF16),
            pltpu.VMEM((2, 2, GD // 2, K - 1, B, B), BF16),
            pltpu.VMEM((2, K, GD, B), jnp.int32),
            pltpu.VMEM((2, K, GD, B), jnp.int32),
            pltpu.VMEM((TR + 2 * GD, 5, B, G), BF16),
            pltpu.VMEM((2, 4, R3, TR * B), BF16),
            pltpu.VMEM((5, TR * B, G), BF16),
            pltpu.VMEM((5, 2, 4, R3, G), F32),
            pltpu.VMEM((5, 4, R3, G), F32),
            pltpu.VMEM((5, R3, G), F32),
            pltpu.VMEM((5, 3, R3 + 16, G), jnp.int16),
            pltpu.VMEM((5, 3, R3 + 16, G), jnp.int16),
            pltpu.VMEM((5, R3, G), F32),
            pltpu.VMEM((5, 2, 32, G), F32),
            dma((3,)),
            dma((2,)), dma((2,)), dma((2,)), dma((2,)), dma((2, 2)), dma((2, 2)), dma((2,)), dma((2,)),
            dma((5,)), dma((5,)), dma((15,)), dma((15,)), dma((10,)), dma((10,)),
        ],
        compiler_params=pltpu.CompilerParams(
            collective_id=0, has_side_effects=True, vmem_limit_bytes=60 * 1024 * 1024
        ),
        cost_estimate=pl.CostEstimate(flops=16_000_000_000, bytes_accessed=8_000_000, transcendentals=0),
    )(a_vals, a_cols.T, send_rows.reshape(2, GD), tentative, p_cols.T)


def solution(mesh):
    placed = (
        P(("dom", "sub"), None, None, None),
        P(("dom", "sub"), None),
        P(("dom", "sub"), None, None),
        P(("dom", "sub"), None, None),
        P(("dom", "sub"), None),
        P(("dom", "sub"), None, None),
    )
    return jax.shard_map(
        on_device, mesh=mesh, in_specs=placed, out_specs=P(("dom", "sub"), None), check_vma=False
    )
```

```python
import jax
import jax.numpy as jnp
from jax import lax
from jax.experimental import pallas as pl
from jax.experimental.pallas import tpu as pltpu
from jax.sharding import PartitionSpec as P

B = 128
K = 4
TR = 32
NCG = 2
GD = 8
G = NCG * B
HB = B // 2
R3 = 96
OMEGA = 0.6
F32 = jnp.float32
BF16 = jnp.bfloat16
MESH = pl.DeviceIdType.MESH


def row_weight(a_v, row, eye):
    diagonal = jnp.sum(jnp.where(eye, a_v[row, 0].astype(F32), 0.0), axis=1, keepdims=True)
    return OMEGA * (1.0 / diagonal)


def smooth_tiles(a_v, t_ext, cols_ref, row, eye, first):
    weight = row_weight(a_v, row, eye)
    tiles = []
    for m in range(first, K):
        product = jnp.dot(a_v[row, m], t_ext[cols_ref[m, row]], preferred_element_type=F32)
        value = weight * product
        value = t_ext[row].astype(F32) - value if m == 0 else -value
        tiles.append(value.astype(BF16))
    return tiles


def doubled(tile, half):
    part = tile[:, half * HB : (half + 1) * HB]
    return jnp.concatenate([part, part], axis=1)


def paired(one, two, half):
    columns = slice(half * HB, (half + 1) * HB)
    return jnp.concatenate([one[:, columns], two[:, columns]], axis=1)


def group_tile(doubles, slots, group):
    wanted = NCG * group + (lax.broadcasted_iota(jnp.int32, (1, B), 1) >= HB).astype(jnp.int32)
    total = None
    for m in range(K):
        if m == 0 and group != 1:
            continue
        ones = jnp.where(slots[m] == wanted, 1.0, 0.0)
        block = jnp.broadcast_to(ones, (16, B)).astype(BF16)
        term = doubles[m] * jnp.concatenate([block] * (B // 16), axis=0)
        total = term if total is None else total + term
    return total


def chunk_of(half, group):
    return (4, half) if group == 4 else (2 * half + group // 2, group % 2)


def put(p_all, row, half, group, tile):
    chunk, at = chunk_of(half, group)
    p_all[row, chunk, :, at * B : (at + 1) * B] = tile


def clear_rows(p_all):
    empty = jnp.zeros((B, B), BF16)
    for first, count, groups in ((0, TR, (0, 4)), (TR, GD, (3, 4)), (TR + GD, GD, (0, 1))):

        def body(j, carry, first=first, groups=groups):
            for group in groups:
                for half in range(2):
                    put(p_all, first + j, half, group, empty)
            return carry

        lax.fori_loop(0, count, body, 0, unroll=2)


def identity_mask():
    return lax.broadcasted_iota(jnp.int32, (B, B), 0) == lax.broadcasted_iota(jnp.int32, (B, B), 1)


def first_tiles(a_v, t_own, lists_ref, s0_send):
    eye = identity_mask()

    def body(j, carry):
        for side in range(2):
            row = lists_ref[side, j]
            product = jnp.dot(a_v[row, 0], t_own[row], preferred_element_type=F32)
            value = t_own[row].astype(F32) - row_weight(a_v, row, eye) * product
            s0_send[side, j] = value.astype(BF16)
        return carry

    lax.fori_loop(0, GD, body, 0, unroll=4)


def send_rows(a_v, t_ext, cols_ref, lists_ref, s_send, start):
    eye = identity_mask()

    def body(pair, carry):
        for side in range(2):
            one, two = (
                smooth_tiles(a_v, t_ext, cols_ref, lists_ref[side, 2 * pair + e], eye, 1) for e in range(2)
            )
            for half in range(2):
                s_send[half, side, pair, 0] = paired(one[0], one[1], half)
                s_send[half, side, pair, 1] = paired(two[0], two[1], half)
                s_send[half, side, pair, 2] = paired(one[2], two[2], half)
            start(side, pair)
        return carry

    lax.fori_loop(0, GD // 2, body, 0, unroll=4)


def own_rows(a_v, t_ext, cols_ref, slots_ref, p_all, p_t, place_of):
    eye = identity_mask()

    def body(row, carry):
        tiles = smooth_tiles(a_v, t_ext, cols_ref, row, eye, 0)
        slots = [slots_ref[m, row] for m in range(K)]
        lanes = pl.ds(pl.multiple_of(row * B, B), B)
        for half in range(2):
            doubles = [doubled(tile, half) for tile in tiles]
            for group in range(3):
                tile = group_tile(doubles, slots, group)
                put(p_all, row, half, group + 1, tile)
                turned = tile.T
                for s in range(2):
                    for c in range(2):
                        first = s * HB + c * 32
                        p_t[c, place_of[2 * s + half], group * 32 : group * 32 + 32, lanes] = turned[
                            first : first + 32
                        ]
        return carry

    lax.fori_loop(0, TR, body, 0, unroll=4)


def halo_rows(half, s0_halo, s_halo, pc_halo, p_all):
    def body(pair, carry):
        for region in range(2):
            for e in range(2):
                j = 2 * pair + e
                both, third = s_halo[half, region, pair, e], s_halo[half, region, pair, 2]
                doubles = [
                    doubled(s0_halo[region, j], half), doubled(both, 0), doubled(both, 1), doubled(third, e),
                ]
                line = pc_halo[region, pl.ds(j, 1), :]
                slots = [jnp.broadcast_to(line[:, m : m + 1], (1, B)) for m in range(K)]
                for group in range(3):
                    put(
                        p_all, TR + region * GD + j, half, group + 2 * region,
                        group_tile(doubles, slots, group),
                    )
        return carry

    lax.fori_loop(0, GD // 2, body, 0, unroll=4)


def place_chunk(n, a_v, cols_ref, p_all, ap):
    first = 1 if n == 4 else 0

    def body(row, carry):
        left = jnp.concatenate([a_v[row, k] for k in range(first, K)], axis=1)
        right = jnp.concatenate([p_all[cols_ref[k, row], n] for k in range(first, K)], axis=0)
        value = jnp.dot(left, right, preferred_element_type=F32)
        ap[n, pl.ds(pl.multiple_of(row * B, B), B), :] = value.astype(BF16)
        return carry

    lax.fori_loop(0, TR, body, 0, unroll=32)


def product_chunk(n, c, p_t, ap, part):
    left = p_t[c].reshape(4 * R3, TR * B)
    value = jnp.dot(left, ap[n], preferred_element_type=F32)
    part[n, c] = value.reshape(4, R3, G)


STEPS = 32000.0
LIFT = 10


def encode(block, coded):
    top = jnp.max(jnp.abs(block), axis=0, keepdims=True)
    exponent = jnp.clip(jnp.ceil(jnp.log2(jnp.maximum(top, 1e-37))), -116.0, 128.0)
    scaled = (block * jnp.exp2(LIFT - exponent)) * (STEPS / 2**LIFT)
    coded[:R3] = jnp.round(scaled).astype(jnp.int32).astype(jnp.int16)
    coded[R3:] = jnp.broadcast_to(exponent, (16, G)).astype(jnp.int32).astype(jnp.int16)


def decode(coded):
    exponent = coded[R3:].astype(jnp.int32).astype(F32)[:1]
    values = coded[:R3].astype(jnp.int32).astype(F32)
    return (values * (2**LIFT / STEPS)) * jnp.exp2(exponent - LIFT)


def kernel(
    a_hbm, cols_ref, lists_ref, t_hbm, slots_ref, out_ref,
    a_v, t_own, t_ext, t_send, s0_send, s0_halo, s_send, s_halo, pc_send, pc_halo,
    p_all, p_t, ap, part, core_in, q, x_out, x_in, fin, y_in,
    load_sem, t_ssem, t_rsem, s0_ssem, s0_rsem, s_ssem, s_rsem, pc_ssem, pc_rsem,
    c_ssem, c_rsem, x_ssem, x_rsem, y_ssem, y_rsem,
):
    dom, sub = lax.axis_index("dom"), lax.axis_index("sub")
    n_dom = lax.axis_size("dom")
    up, down = lax.rem(dom + 1, n_dom), lax.rem(dom + n_dom - 1, n_dom)
    x, core = sub // 2, lax.rem(sub, 2)
    xa = x + 1 - 2 * lax.rem(x, 2)
    xb = 3 - x
    xo = lax.rem(x + 2, 4)
    to_up, to_down = (up, sub), (down, sub)
    to_core = (dom, 2 * x + 1 - core)
    to_ring = tuple((dom, 2 * chip + core) for chip in (xa, xb, xo))

    barrier = pltpu.get_barrier_semaphore()
    for device in (to_up, to_down, to_core) + to_ring:
        pl.semaphore_signal(barrier, inc=1, device_id=device, device_id_type=MESH)

    load_own = pltpu.make_async_copy(t_hbm, t_own, load_sem.at[0])
    load_ext = pltpu.make_async_copy(t_hbm, t_ext.at[pl.ds(0, TR)], load_sem.at[1])
    load_a = pltpu.make_async_copy(a_hbm, a_v, load_sem.at[2])
    load_own.start()
    load_a.start()
    load_ext.start()

    def remote(src, dst, ssem, rsem, device):
        return pltpu.make_async_remote_copy(
            src_ref=src, dst_ref=dst, send_sem=ssem, recv_sem=rsem,
            device_id=device, device_id_type=MESH,
        )

    load_own.wait()

    def gather_row(j, carry):
        for side in range(2):
            t_send[side, j] = t_own[lists_ref[side, j]]
        return carry

    lax.fori_loop(0, GD, gather_row, 0, unroll=4)

    lane = lax.broadcasted_iota(jnp.int32, (1, B), 1)
    for side in range(2):
        for j in range(GD):
            row = lists_ref[side, j]
            line = jnp.full((1, B), slots_ref[0, row], jnp.int32)
            for m in range(1, K):
                line = jnp.where(lane == m, slots_ref[m, row], line)
            pc_send[side, j : j + 1, :] = line

    load_a.wait()
    first_tiles(a_v, t_own, lists_ref, s0_send)
    pl.semaphore_wait(barrier, 6)

    early = []
    for send, halo, ssem, rsem in (
        (t_send, None, t_ssem, t_rsem), (pc_send, pc_halo, pc_ssem, pc_rsem), (s0_send, s0_halo, s0_ssem, s0_rsem),
    ):
        for region, device in ((0, to_up), (1, to_down)):
            target = t_ext.at[pl.ds(TR + GD * region, GD)] if halo is None else halo.at[region]
            early.append(remote(send.at[1 - region], target, ssem.at[region], rsem.at[region], device))
            early[-1].start()

    clear_rows(p_all)
    load_ext.wait()
    early[0].wait_recv()
    early[1].wait_recv()

    def start_pair(side, pair):
        remote(
            s_send.at[0, side, pair], s_halo.at[0, 1 - side, pair], s_ssem.at[0, side], s_rsem.at[0, side],
            to_up if side == 1 else to_down,
        ).start()

    send_rows(a_v, t_ext, cols_ref, lists_ref, s_send, start_pair)

    def side_copy(half, side):
        return remote(
            s_send.at[half, side], s_halo.at[half, 1 - side], s_ssem.at[half, side], s_rsem.at[half, side],
            to_up if side == 1 else to_down,
        )

    s_copies = [[side_copy(half, side) for side in range(2)] for half in range(2)]

    place_of = [
        jnp.where(t == xa, 0, jnp.where(t == xb, 1, jnp.where(t == xo, 2, 3))) for t in range(4)
    ]
    own_rows(a_v, t_ext, cols_ref, slots_ref, p_all, p_t, place_of)
    for copy in s_copies[1]:
        copy.start()

    core_copies, x_copies, y_copies = [], [None] * 15, []

    def begin(copies, *args):
        copies.append(remote(*args))
        copies[-1].start()

    def core_stage(n):
        core_copies[n].wait_recv()
        for t in (2, 0, 1):
            encode(part[n, core, t] + core_in[n, t], x_out.at[n, t])
        for t in (2, 0, 1):
            i = 3 * n + t
            x_copies[i] = remote(x_out.at[n, t], x_in.at[n, t], x_ssem.at[i], x_rsem.at[i], to_ring[t])
            x_copies[i].start()
        q[n] = part[n, core, 3] + core_in[n, 3]

    def x_stage(n):
        for t in range(3):
            x_copies[3 * n + t].wait_recv()
        total = (q[n] + decode(x_in.at[n, 0])) + (decode(x_in.at[n, 1]) + decode(x_in.at[n, 2]))
        fin[1, n], fin[2, n], fin[0, n] = total[:32], total[32:64], total[64:]

    def y_stage(first, count):
        chunks = pl.ds(first, count)
        for region, device in ((0, to_up), (1, to_down)):
            i = 2 * first + region
            begin(
                y_copies, fin.at[region, chunks], y_in.at[region, chunks], y_ssem.at[i], y_rsem.at[i], device
            )

    def place(n):
        place_chunk(n, a_v, cols_ref, p_all, ap)

    def product(n):
        for c in range(2):
            product_chunk(n, c, p_t, ap, part)
        begin(core_copies, part.at[n, 1 - core], core_in.at[n], c_ssem.at[n], c_rsem.at[n], to_core)

    for copy in early[2:] + s_copies[0]:
        copy.wait_recv()
    halo_rows(0, s0_halo, s_halo, pc_halo, p_all)
    place(0)
    product(0)
    place(1)
    core_stage(0)
    product(1)
    for copy in s_copies[1]:
        copy.wait_recv()
    halo_rows(1, s0_halo, s_halo, pc_halo, p_all)
    place(2)
    core_stage(1)
    product(2)
    place(3)
    core_stage(2)
    product(3)
    place(4)
    core_stage(3)
    product(4)
    x_stage(0)
    core_stage(4)
    x_stage(1)
    x_stage(2)
    x_stage(3)
    y_stage(0, 4)
    x_stage(4)
    y_stage(4, 1)
    for copy in early + s_copies[0] + s_copies[1] + core_copies + x_copies + y_copies:
        copy.wait_send()
    for copy in y_copies:
        copy.wait_recv()

    def columns(array, half, group):
        chunk, at = chunk_of(half, group)
        return array(chunk)[:, at * B : (at + 1) * B]

    for g in range(7):
        halves = []
        for half in range(2):
            total = None
            for group, array in (
                (g - 1, lambda n: fin[2, n]),
                (g, lambda n: jnp.where(dom > 0, y_in[0, n], 0.0)),
                (g - 2, lambda n: jnp.where(dom < n_dom - 1, y_in[1, n], 0.0)),
            ):
                if 0 <= group < 5:
                    value = columns(array, half, group)
                    total = value if total is None else total + value
            halves.append(total)
        for s in range(2):
            out_ref[:, g * G + s * B : g * G + (s + 1) * B] = paired(halves[0], halves[1], s)


def on_device(a_vals, a_cols, send_rows, tentative, p_cols, ap_cols):
    hbm = pl.BlockSpec(memory_space=pl.ANY)
    smem = pl.BlockSpec(memory_space=pltpu.SMEM)
    dma = pltpu.SemaphoreType.DMA
    return pl.pallas_call(
        kernel,
        out_shape=jax.ShapeDtypeStruct((32, 7 * G), F32),
        in_specs=[hbm, smem, smem, hbm, smem],
        out_specs=pl.BlockSpec(memory_space=pltpu.VMEM),
        scratch_shapes=[
            pltpu.VMEM((TR, K, B, B), BF16),
            pltpu.VMEM((TR, B, B), BF16),
            pltpu.VMEM((TR + 2 * GD, B, B), BF16),
            pltpu.VMEM((2, GD, B, B), BF16),
            pltpu.VMEM((2, GD, B, B), BF16),
            pltpu.VMEM((2, GD, B, B), BF16),
            pltpu.VMEM((2, 2, GD // 2, K - 1, B, B), BF16),
            pltpu.VMEM((2, 2, GD // 2, K - 1, B, B), BF16),
            pltpu.VMEM((2, GD, B), jnp.int32),
            pltpu.VMEM((2, GD, B), jnp.int32),
            pltpu.VMEM((TR + 2 * GD, 5, B, G), BF16),
            pltpu.VMEM((2, 4, R3, TR * B), BF16),
            pltpu.VMEM((5, TR * B, G), BF16),
            pltpu.VMEM((5, 2, 4, R3, G), F32),
            pltpu.VMEM((5, 4, R3, G), F32),
            pltpu.VMEM((5, R3, G), F32),
            pltpu.VMEM((5, 3, R3 + 16, G), jnp.int16),
            pltpu.VMEM((5, 3, R3 + 16, G), jnp.int16),
            pltpu.VMEM((3, 5, 32, G), F32),
            pltpu.VMEM((2, 5, 32, G), F32),
            dma((3,)),
            dma((2,)), dma((2,)), dma((2,)), dma((2,)), dma((2, 2)), dma((2, 2)), dma((2,)), dma((2,)),
            dma((5,)), dma((5,)), dma((15,)), dma((15,)), dma((10,)), dma((10,)),
        ],
        compiler_params=pltpu.CompilerParams(
            collective_id=0, has_side_effects=True, vmem_limit_bytes=60 * 1024 * 1024
        ),
        cost_estimate=pl.CostEstimate(flops=16_000_000_000, bytes_accessed=8_000_000, transcendentals=0),
    )(a_vals, a_cols.T, send_rows.reshape(2, GD), tentative, p_cols.T)


def solution(mesh):
    placed = (
        P(("dom", "sub"), None, None, None),
        P(("dom", "sub"), None),
        P(("dom", "sub"), None, None),
        P(("dom", "sub"), None, None),
        P(("dom", "sub"), None),
        P(("dom", "sub"), None, None),
    )
    return jax.shard_map(
        on_device, mesh=mesh, in_specs=placed, out_specs=P(("dom", "sub"), None), check_vma=False
    )
```

```python
import jax
import jax.numpy as jnp
from jax import lax
from jax.experimental import pallas as pl
from jax.experimental.pallas import tpu as pltpu
from jax.sharding import PartitionSpec as P

B = 128
K = 4
TR = 32
NCG = 2
GD = 8
G = NCG * B
HB = B // 2
R3 = 96
OMEGA = 0.6
F32 = jnp.float32
BF16 = jnp.bfloat16
MESH = pl.DeviceIdType.MESH


def row_weight(a_v, row, eye):
    diagonal = jnp.sum(jnp.where(eye, a_v[row, 0].astype(F32), 0.0), axis=1, keepdims=True)
    return OMEGA * (1.0 / diagonal)


def smooth_tiles(a_v, t_ext, cols_ref, row, eye, first):
    weight = row_weight(a_v, row, eye)
    tiles = []
    for m in range(first, K):
        product = jnp.dot(a_v[row, m], t_ext[cols_ref[m, row]], preferred_element_type=F32)
        value = weight * product
        value = t_ext[row].astype(F32) - value if m == 0 else -value
        tiles.append(value.astype(BF16))
    return tiles


def doubled(tile, half):
    part = tile[:, half * HB : (half + 1) * HB]
    return jnp.concatenate([part, part], axis=1)


def paired(one, two, half):
    columns = slice(half * HB, (half + 1) * HB)
    return jnp.concatenate([one[:, columns], two[:, columns]], axis=1)


def group_tile(doubles, slots, group):
    wanted = NCG * group + (lax.broadcasted_iota(jnp.int32, (1, B), 1) >= HB).astype(jnp.int32)
    total = None
    for m in range(K):
        if m == 0 and group != 1:
            continue
        ones = jnp.where(slots[m] == wanted, 1.0, 0.0)
        block = jnp.broadcast_to(ones, (16, B)).astype(BF16)
        term = doubles[m] * jnp.concatenate([block] * (B // 16), axis=0)
        total = term if total is None else total + term
    return total


def chunk_of(half, group):
    return (4, half) if group == 4 else (2 * half + group // 2, group % 2)


def put(p_all, row, half, group, tile):
    chunk, at = chunk_of(half, group)
    p_all[row, chunk, :, at * B : (at + 1) * B] = tile


def clear_rows(p_all):
    empty = jnp.zeros((B, B), BF16)
    for first, count, groups in ((0, TR, (0, 4)), (TR, GD, (3, 4)), (TR + GD, GD, (0, 1))):

        def body(j, carry, first=first, groups=groups):
            for group in groups:
                for half in range(2):
                    put(p_all, first + j, half, group, empty)
            return carry

        lax.fori_loop(0, count, body, 0, unroll=2)


def identity_mask():
    return lax.broadcasted_iota(jnp.int32, (B, B), 0) == lax.broadcasted_iota(jnp.int32, (B, B), 1)


def first_tiles(a_v, t_own, lists_ref, s0_send):
    eye = identity_mask()

    def body(j, carry):
        for side in range(2):
            row = lists_ref[side, j]
            product = jnp.dot(a_v[row, 0], t_own[row], preferred_element_type=F32)
            value = t_own[row].astype(F32) - row_weight(a_v, row, eye) * product
            s0_send[side, j] = value.astype(BF16)
        return carry

    lax.fori_loop(0, GD, body, 0, unroll=4)


def send_rows(a_v, t_ext, cols_ref, lists_ref, s_send, start):
    eye = identity_mask()

    def body(pair, carry):
        for side in range(2):
            one, two = (
                smooth_tiles(a_v, t_ext, cols_ref, lists_ref[side, 2 * pair + e], eye, 1) for e in range(2)
            )
            for half in range(2):
                s_send[half, side, pair, 0] = paired(one[0], one[1], half)
                s_send[half, side, pair, 1] = paired(two[0], two[1], half)
                s_send[half, side, pair, 2] = paired(one[2], two[2], half)
            start(side, pair)
        return carry

    lax.fori_loop(0, GD // 2, body, 0, unroll=4)


def own_rows(a_v, t_ext, cols_ref, slots_ref, p_all, p_t, place_of):
    eye = identity_mask()

    def body(row, carry):
        tiles = smooth_tiles(a_v, t_ext, cols_ref, row, eye, 0)
        slots = [slots_ref[m, row] for m in range(K)]
        lanes = pl.ds(pl.multiple_of(row * B, B), B)
        for half in range(2):
            doubles = [doubled(tile, half) for tile in tiles]
            for group in range(3):
                tile = group_tile(doubles, slots, group)
                put(p_all, row, half, group + 1, tile)
                turned = tile.T
                for s in range(2):
                    for c in range(2):
                        first = s * HB + c * 32
                        p_t[c, place_of[2 * s + half], group * 32 : group * 32 + 32, lanes] = turned[
                            first : first + 32
                        ]
        return carry

    lax.fori_loop(0, TR, body, 0, unroll=4)


def halo_rows(half, s0_halo, s_halo, pc_halo, p_all):
    def body(pair, carry):
        for region in range(2):
            for e in range(2):
                j = 2 * pair + e
                both, third = s_halo[half, region, pair, e], s_halo[half, region, pair, 2]
                doubles = [
                    doubled(s0_halo[region, j], half), doubled(both, 0), doubled(both, 1), doubled(third, e),
                ]
                line = pc_halo[region, pl.ds(j, 1), :]
                slots = [jnp.broadcast_to(line[:, m : m + 1], (1, B)) for m in range(K)]
                for group in range(3):
                    put(
                        p_all, TR + region * GD + j, half, group + 2 * region,
                        group_tile(doubles, slots, group),
                    )
        return carry

    lax.fori_loop(0, GD // 2, body, 0, unroll=4)


def place_chunk(n, a_v, cols_ref, p_all, ap):
    first = 1 if n == 4 else 0

    def body(row, carry):
        left = jnp.concatenate([a_v[row, k] for k in range(first, K)], axis=1)
        right = jnp.concatenate([p_all[cols_ref[k, row], n] for k in range(first, K)], axis=0)
        value = jnp.dot(left, right, preferred_element_type=F32)
        ap[n, pl.ds(pl.multiple_of(row * B, B), B), :] = value.astype(BF16)
        return carry

    lax.fori_loop(0, TR, body, 0, unroll=32)


def product_chunk(n, c, p_t, ap, part):
    left = p_t[c].reshape(4 * R3, TR * B)
    value = jnp.dot(left, ap[n], preferred_element_type=F32)
    part[n, c] = value.reshape(4, R3, G)


STEPS = 32000.0
LIFT = 10


def encode(block, coded):
    top = jnp.max(jnp.abs(block), axis=0, keepdims=True)
    exponent = jnp.clip(jnp.ceil(jnp.log2(jnp.maximum(top, 1e-37))), -116.0, 128.0)
    scaled = (block * jnp.exp2(LIFT - exponent)) * (STEPS / 2**LIFT)
    coded[:R3] = jnp.round(scaled).astype(jnp.int32).astype(jnp.int16)
    coded[R3:] = jnp.broadcast_to(exponent, (16, G)).astype(jnp.int32).astype(jnp.int16)


def decode(coded):
    exponent = coded[R3:].astype(jnp.int32).astype(F32)[:1]
    values = coded[:R3].astype(jnp.int32).astype(F32)
    return (values * (2**LIFT / STEPS)) * jnp.exp2(exponent - LIFT)


def kernel(
    a_hbm, cols_hbm, lists_hbm, t_hbm, slots_hbm, out_ref,
    cols_ref, lists_ref, slots_ref, a_v, t_own, t_ext, t_send, s0_send, s0_halo, s_send, s_halo, pc_send, pc_halo,
    p_all, p_t, ap, part, core_in, q, x_out, x_in, fin, y_in,
    load_sem, t_ssem, t_rsem, s0_ssem, s0_rsem, s_ssem, s_rsem, pc_ssem, pc_rsem,
    c_ssem, c_rsem, x_ssem, x_rsem, y_ssem, y_rsem,
):
    dom, sub = lax.axis_index("dom"), lax.axis_index("sub")
    n_dom = lax.axis_size("dom")
    up, down = lax.rem(dom + 1, n_dom), lax.rem(dom + n_dom - 1, n_dom)
    x, core = sub // 2, lax.rem(sub, 2)
    xa = x + 1 - 2 * lax.rem(x, 2)
    xb = 3 - x
    xo = lax.rem(x + 2, 4)
    to_up, to_down = (up, sub), (down, sub)
    to_core = (dom, 2 * x + 1 - core)
    to_ring = tuple((dom, 2 * chip + core) for chip in (xa, xb, xo))

    barrier = pltpu.get_barrier_semaphore()
    for device in (to_up, to_down, to_core) + to_ring:
        pl.semaphore_signal(barrier, inc=1, device_id=device, device_id_type=MESH)

    load_own = pltpu.make_async_copy(t_hbm, t_own, load_sem.at[0])
    load_ext = pltpu.make_async_copy(t_hbm, t_ext.at[pl.ds(0, TR)], load_sem.at[1])
    load_a = pltpu.make_async_copy(a_hbm, a_v, load_sem.at[2])
    load_lists = pltpu.make_async_copy(lists_hbm, lists_ref, load_sem.at[3])
    load_cols = pltpu.make_async_copy(cols_hbm, cols_ref, load_sem.at[4])
    load_slots = pltpu.make_async_copy(slots_hbm, slots_ref, load_sem.at[5])
    load_lists.start()
    load_own.start()
    load_cols.start()
    load_slots.start()
    load_a.start()
    load_ext.start()

    def remote(src, dst, ssem, rsem, device):
        return pltpu.make_async_remote_copy(
            src_ref=src, dst_ref=dst, send_sem=ssem, recv_sem=rsem,
            device_id=device, device_id_type=MESH,
        )

    load_lists.wait()
    load_cols.wait()
    load_slots.wait()
    load_own.wait()

    def gather_row(j, carry):
        for side in range(2):
            t_send[side, j] = t_own[lists_ref[side, j]]
        return carry

    lax.fori_loop(0, GD, gather_row, 0, unroll=4)

    lane = lax.broadcasted_iota(jnp.int32, (1, B), 1)
    for side in range(2):
        for j in range(GD):
            row = lists_ref[side, j]
            line = jnp.full((1, B), slots_ref[0, row], jnp.int32)
            for m in range(1, K):
                line = jnp.where(lane == m, slots_ref[m, row], line)
            pc_send[side, j : j + 1, :] = line

    load_a.wait()
    first_tiles(a_v, t_own, lists_ref, s0_send)
    pl.semaphore_wait(barrier, 6)

    early = []
    for send, halo, ssem, rsem in (
        (t_send, None, t_ssem, t_rsem), (pc_send, pc_halo, pc_ssem, pc_rsem), (s0_send, s0_halo, s0_ssem, s0_rsem),
    ):
        for region, device in ((0, to_up), (1, to_down)):
            target = t_ext.at[pl.ds(TR + GD * region, GD)] if halo is None else halo.at[region]
            early.append(remote(send.at[1 - region], target, ssem.at[region], rsem.at[region], device))
            early[-1].start()

    clear_rows(p_all)
    load_ext.wait()
    early[0].wait_recv()
    early[1].wait_recv()

    def start_pair(side, pair):
        remote(
            s_send.at[0, side, pair], s_halo.at[0, 1 - side, pair], s_ssem.at[0, side], s_rsem.at[0, side],
            to_up if side == 1 else to_down,
        ).start()

    send_rows(a_v, t_ext, cols_ref, lists_ref, s_send, start_pair)

    def side_copy(half, side):
        return remote(
            s_send.at[half, side], s_halo.at[half, 1 - side], s_ssem.at[half, side], s_rsem.at[half, side],
            to_up if side == 1 else to_down,
        )

    s_copies = [[side_copy(half, side) for side in range(2)] for half in range(2)]

    place_of = [
        jnp.where(t == xa, 0, jnp.where(t == xb, 1, jnp.where(t == xo, 2, 3))) for t in range(4)
    ]
    own_rows(a_v, t_ext, cols_ref, slots_ref, p_all, p_t, place_of)
    for copy in s_copies[1]:
        copy.start()

    core_copies, x_copies, y_copies = [], [None] * 15, []

    def begin(copies, *args):
        copies.append(remote(*args))
        copies[-1].start()

    def core_stage(n):
        core_copies[n].wait_recv()
        for t in (2, 0, 1):
            encode(part[n, core, t] + core_in[n, t], x_out.at[n, t])
        for t in (2, 0, 1):
            i = 3 * n + t
            x_copies[i] = remote(x_out.at[n, t], x_in.at[n, t], x_ssem.at[i], x_rsem.at[i], to_ring[t])
            x_copies[i].start()
        q[n] = part[n, core, 3] + core_in[n, 3]

    def x_stage(n):
        for t in range(3):
            x_copies[3 * n + t].wait_recv()
        total = (q[n] + decode(x_in.at[n, 0])) + (decode(x_in.at[n, 1]) + decode(x_in.at[n, 2]))
        fin[1, n], fin[2, n], fin[0, n] = total[:32], total[32:64], total[64:]

    def y_stage(first, count):
        chunks = pl.ds(first, count)
        for region, device in ((0, to_up), (1, to_down)):
            i = 2 * first + region
            begin(
                y_copies, fin.at[region, chunks], y_in.at[region, chunks], y_ssem.at[i], y_rsem.at[i], device
            )

    def place(n):
        place_chunk(n, a_v, cols_ref, p_all, ap)

    def product(n):
        for c in range(2):
            product_chunk(n, c, p_t, ap, part)
        begin(core_copies, part.at[n, 1 - core], core_in.at[n], c_ssem.at[n], c_rsem.at[n], to_core)

    for copy in early[2:] + s_copies[0]:
        copy.wait_recv()
    halo_rows(0, s0_halo, s_halo, pc_halo, p_all)
    place(0)
    product(0)
    place(1)
    core_stage(0)
    product(1)
    for copy in s_copies[1]:
        copy.wait_recv()
    halo_rows(1, s0_halo, s_halo, pc_halo, p_all)
    place(2)
    core_stage(1)
    product(2)
    place(3)
    core_stage(2)
    product(3)
    place(4)
    core_stage(3)
    product(4)
    x_stage(0)
    core_stage(4)
    x_stage(1)
    x_stage(2)
    x_stage(3)
    y_stage(0, 4)
    x_stage(4)
    y_stage(4, 1)
    for copy in early + s_copies[0] + s_copies[1] + core_copies + x_copies + y_copies:
        copy.wait_send()
    for copy in y_copies:
        copy.wait_recv()

    def columns(array, half, group):
        chunk, at = chunk_of(half, group)
        return array(chunk)[:, at * B : (at + 1) * B]

    for g in range(7):
        halves = []
        for half in range(2):
            total = None
            for group, array in (
                (g - 1, lambda n: fin[2, n]),
                (g, lambda n: jnp.where(dom > 0, y_in[0, n], 0.0)),
                (g - 2, lambda n: jnp.where(dom < n_dom - 1, y_in[1, n], 0.0)),
            ):
                if 0 <= group < 5:
                    value = columns(array, half, group)
                    total = value if total is None else total + value
            halves.append(total)
        for s in range(2):
            out_ref[:, g * G + s * B : g * G + (s + 1) * B] = paired(halves[0], halves[1], s)


def on_device(a_vals, a_cols, send_rows, tentative, p_cols, ap_cols):
    hbm = pl.BlockSpec(memory_space=pl.ANY)
    dma = pltpu.SemaphoreType.DMA
    return pl.pallas_call(
        kernel,
        out_shape=jax.ShapeDtypeStruct((32, 7 * G), F32),
        in_specs=[hbm] * 5,
        out_specs=pl.BlockSpec(memory_space=pltpu.VMEM),
        scratch_shapes=[
            pltpu.SMEM((K, TR), jnp.int32), pltpu.SMEM((2, GD), jnp.int32), pltpu.SMEM((K, TR), jnp.int32),
            pltpu.VMEM((TR, K, B, B), BF16),
            pltpu.VMEM((TR, B, B), BF16),
            pltpu.VMEM((TR + 2 * GD, B, B), BF16),
            pltpu.VMEM((2, GD, B, B), BF16),
            pltpu.VMEM((2, GD, B, B), BF16),
            pltpu.VMEM((2, GD, B, B), BF16),
            pltpu.VMEM((2, 2, GD // 2, K - 1, B, B), BF16),
            pltpu.VMEM((2, 2, GD // 2, K - 1, B, B), BF16),
            pltpu.VMEM((2, GD, B), jnp.int32),
            pltpu.VMEM((2, GD, B), jnp.int32),
            pltpu.VMEM((TR + 2 * GD, 5, B, G), BF16),
            pltpu.VMEM((2, 4, R3, TR * B), BF16),
            pltpu.VMEM((5, TR * B, G), BF16),
            pltpu.VMEM((5, 2, 4, R3, G), F32),
            pltpu.VMEM((5, 4, R3, G), F32),
            pltpu.VMEM((5, R3, G), F32),
            pltpu.VMEM((5, 3, R3 + 16, G), jnp.int16),
            pltpu.VMEM((5, 3, R3 + 16, G), jnp.int16),
            pltpu.VMEM((3, 5, 32, G), F32),
            pltpu.VMEM((2, 5, 32, G), F32),
            dma((6,)),
            dma((2,)), dma((2,)), dma((2,)), dma((2,)), dma((2, 2)), dma((2, 2)), dma((2,)), dma((2,)),
            dma((5,)), dma((5,)), dma((15,)), dma((15,)), dma((10,)), dma((10,)),
        ],
        compiler_params=pltpu.CompilerParams(
            collective_id=0, has_side_effects=True, vmem_limit_bytes=60 * 1024 * 1024
        ),
        cost_estimate=pl.CostEstimate(flops=16_000_000_000, bytes_accessed=8_000_000, transcendentals=0),
    )(a_vals, a_cols.T, send_rows.reshape(2, GD), tentative, p_cols.T)


def solution(mesh):
    placed = (
        P(("dom", "sub"), None, None, None),
        P(("dom", "sub"), None),
        P(("dom", "sub"), None, None),
        P(("dom", "sub"), None, None),
        P(("dom", "sub"), None),
        P(("dom", "sub"), None, None),
    )
    return jax.shard_map(
        on_device, mesh=mesh, in_specs=placed, out_specs=P(("dom", "sub"), None), check_vma=False
    )
```

```python
import jax
import jax.numpy as jnp
from jax import lax
from jax.experimental import pallas as pl
from jax.experimental.pallas import tpu as pltpu
from jax.sharding import PartitionSpec as P

B = 128
K = 4
TR = 32
NCG = 2
GD = 8
G = NCG * B
HB = B // 2
R3 = 96
OMEGA = 0.6
F32 = jnp.float32
BF16 = jnp.bfloat16
MESH = pl.DeviceIdType.MESH


def row_weight(a_v, row, eye):
    diagonal = jnp.sum(jnp.where(eye, a_v[row, 0].astype(F32), 0.0), axis=1, keepdims=True)
    return OMEGA * (1.0 / diagonal)


def smooth_tiles(a_v, t_ext, cols_ref, row, eye, first):
    weight = row_weight(a_v, row, eye)
    tiles = []
    for m in range(first, K):
        product = jnp.dot(a_v[row, m], t_ext[cols_ref[m, row]], preferred_element_type=F32)
        value = weight * product
        value = t_ext[row].astype(F32) - value if m == 0 else -value
        tiles.append(value.astype(BF16))
    return tiles


def doubled(tile, half):
    part = tile[:, half * HB : (half + 1) * HB]
    return jnp.concatenate([part, part], axis=1)


def paired(one, two, half):
    columns = slice(half * HB, (half + 1) * HB)
    return jnp.concatenate([one[:, columns], two[:, columns]], axis=1)


def group_tile(doubles, slots, group):
    wanted = NCG * group + (lax.broadcasted_iota(jnp.int32, (1, B), 1) >= HB).astype(jnp.int32)
    total = None
    for m in range(K):
        if m == 0 and group != 1:
            continue
        ones = jnp.where(slots[m] == wanted, 1.0, 0.0)
        block = jnp.broadcast_to(ones, (16, B)).astype(BF16)
        term = doubles[m] * jnp.concatenate([block] * (B // 16), axis=0)
        total = term if total is None else total + term
    return total


def chunk_of(half, group):
    return (4, half) if group == 4 else (2 * half + group // 2, group % 2)


def put(p_all, row, half, group, tile):
    chunk, at = chunk_of(half, group)
    p_all[row, chunk, :, at * B : (at + 1) * B] = tile


def clear_rows(p_all):
    empty = jnp.zeros((B, B), BF16)
    for first, count, groups in ((0, TR, (0, 4)), (TR, GD, (3, 4)), (TR + GD, GD, (0, 1))):

        def body(j, carry, first=first, groups=groups):
            for group in groups:
                for half in range(2):
                    put(p_all, first + j, half, group, empty)
            return carry

        lax.fori_loop(0, count, body, 0, unroll=2)


def identity_mask():
    return lax.broadcasted_iota(jnp.int32, (B, B), 0) == lax.broadcasted_iota(jnp.int32, (B, B), 1)


def first_tiles(a_v, t_own, lists_ref, s0_send):
    eye = identity_mask()

    def body(j, carry):
        for side in range(2):
            row = lists_ref[side, j]
            product = jnp.dot(a_v[row, 0], t_own[row], preferred_element_type=F32)
            value = t_own[row].astype(F32) - row_weight(a_v, row, eye) * product
            s0_send[side, j] = value.astype(BF16)
        return carry

    lax.fori_loop(0, GD, body, 0, unroll=4)


def send_rows(a_v, t_ext, cols_ref, lists_ref, s_send, start):
    eye = identity_mask()

    def body(pair, carry):
        for side in range(2):
            one, two = (
                smooth_tiles(a_v, t_ext, cols_ref, lists_ref[side, 2 * pair + e], eye, 1) for e in range(2)
            )
            for half in range(2):
                s_send[half, side, pair, 0] = paired(one[0], one[1], half)
                s_send[half, side, pair, 1] = paired(two[0], two[1], half)
                s_send[half, side, pair, 2] = paired(one[2], two[2], half)
            start(side, pair)
        return carry

    lax.fori_loop(0, GD // 2, body, 0, unroll=4)


def own_rows(a_v, t_ext, cols_ref, slots_ref, p_all, p_t, place_of):
    eye = identity_mask()

    def body(row, carry):
        tiles = smooth_tiles(a_v, t_ext, cols_ref, row, eye, 0)
        slots = [slots_ref[m, row] for m in range(K)]
        lanes = pl.ds(pl.multiple_of(row * B, B), B)
        for half in range(2):
            doubles = [doubled(tile, half) for tile in tiles]
            for group in range(3):
                tile = group_tile(doubles, slots, group)
                put(p_all, row, half, group + 1, tile)
                turned = tile.T
                for s in range(2):
                    for c in range(2):
                        first = s * HB + c * 32
                        p_t[c, place_of[2 * s + half], group * 32 : group * 32 + 32, lanes] = turned[
                            first : first + 32
                        ]
        return carry

    lax.fori_loop(0, TR, body, 0, unroll=4)


def halo_rows(half, s0_halo, s_halo, pc_halo, p_all):
    def body(pair, carry):
        for region in range(2):
            for e in range(2):
                j = 2 * pair + e
                both, third = s_halo[half, region, pair, e], s_halo[half, region, pair, 2]
                doubles = [
                    doubled(s0_halo[region, j], half), doubled(both, 0), doubled(both, 1), doubled(third, e),
                ]
                line = pc_halo[region, pl.ds(j, 1), :]
                slots = [jnp.broadcast_to(line[:, m : m + 1], (1, B)) for m in range(K)]
                for group in range(3):
                    put(
                        p_all, TR + region * GD + j, half, group + 2 * region,
                        group_tile(doubles, slots, group),
                    )
        return carry

    lax.fori_loop(0, GD // 2, body, 0, unroll=4)


def place_chunk(n, a_v, cols_ref, p_all, ap):
    first = 1 if n == 4 else 0

    def body(row, carry):
        left = jnp.concatenate([a_v[row, k] for k in range(first, K)], axis=1)
        right = jnp.concatenate([p_all[cols_ref[k, row], n] for k in range(first, K)], axis=0)
        value = jnp.dot(left, right, preferred_element_type=F32)
        ap[n, pl.ds(pl.multiple_of(row * B, B), B), :] = value.astype(BF16)
        return carry

    lax.fori_loop(0, TR, body, 0, unroll=32)


def product_chunk(n, c, p_t, ap, part):
    left = p_t[c].reshape(4 * R3, TR * B)
    value = jnp.dot(left, ap[n], preferred_element_type=F32)
    part[n, c] = value.reshape(4, R3, G)


STEPS = 32000.0
LIFT = 10


def encode(block, coded):
    top = jnp.max(jnp.abs(block), axis=0, keepdims=True)
    exponent = jnp.clip(jnp.ceil(jnp.log2(jnp.maximum(top, 1e-37))), -116.0, 128.0)
    scaled = (block * jnp.exp2(LIFT - exponent)) * (STEPS / 2**LIFT)
    coded[:R3] = jnp.round(scaled).astype(jnp.int32).astype(jnp.int16)
    coded[R3:] = jnp.broadcast_to(exponent, (16, G)).astype(jnp.int32).astype(jnp.int16)


def decode(coded):
    exponent = coded[R3:].astype(jnp.int32).astype(F32)[:1]
    values = coded[:R3].astype(jnp.int32).astype(F32)
    return (values * (2**LIFT / STEPS)) * jnp.exp2(exponent - LIFT)


def kernel(
    a_hbm, cols_hbm, lists_hbm, t_hbm, slots_hbm, out_ref,
    cols_ref, lists_ref, slots_ref, a_v, t_own, t_ext, t_send, s0_send, s0_halo, s_send, s_halo, pc_send, pc_halo,
    p_all, p_t, ap, part, core_in, q, x_out, x_in, fin, y_in,
    load_sem, t_ssem, t_rsem, s0_ssem, s0_rsem, s_ssem, s_rsem, pc_ssem, pc_rsem,
    c_ssem, c_rsem, x_ssem, x_rsem, y_ssem, y_rsem,
):
    dom, sub = lax.axis_index("dom"), lax.axis_index("sub")
    n_dom = lax.axis_size("dom")
    up, down = lax.rem(dom + 1, n_dom), lax.rem(dom + n_dom - 1, n_dom)
    x, core = sub // 2, lax.rem(sub, 2)
    xa = x + 1 - 2 * lax.rem(x, 2)
    xb = 3 - x
    xo = lax.rem(x + 2, 4)
    to_up, to_down = (up, sub), (down, sub)
    to_core = (dom, 2 * x + 1 - core)
    to_ring = tuple((dom, 2 * chip + core) for chip in (xa, xb, xo))

    barrier = pltpu.get_barrier_semaphore()
    for device in (to_up, to_down, to_core) + to_ring:
        pl.semaphore_signal(barrier, inc=1, device_id=device, device_id_type=MESH)

    load_own = pltpu.make_async_copy(t_hbm, t_own, load_sem.at[0])
    load_ext = pltpu.make_async_copy(t_hbm, t_ext.at[pl.ds(0, TR)], load_sem.at[1])
    load_a = pltpu.make_async_copy(a_hbm, a_v, load_sem.at[2])
    load_lists = pltpu.make_async_copy(lists_hbm, lists_ref, load_sem.at[3])
    load_cols = pltpu.make_async_copy(cols_hbm, cols_ref, load_sem.at[4])
    load_slots = pltpu.make_async_copy(slots_hbm, slots_ref, load_sem.at[5])
    load_lists.start()
    load_own.start()
    load_cols.start()
    load_slots.start()
    load_a.start()
    load_ext.start()

    def remote(src, dst, ssem, rsem, device):
        return pltpu.make_async_remote_copy(
            src_ref=src, dst_ref=dst, send_sem=ssem, recv_sem=rsem,
            device_id=device, device_id_type=MESH,
        )

    load_lists.wait()
    load_own.wait()

    def gather_row(j, carry):
        for side in range(2):
            t_send[side, j] = t_own[lists_ref[side, j]]
        return carry

    lax.fori_loop(0, GD, gather_row, 0, unroll=4)

    lane = lax.broadcasted_iota(jnp.int32, (1, B), 1)
    load_slots.wait()
    for side in range(2):
        for j in range(GD):
            row = lists_ref[side, j]
            line = jnp.full((1, B), slots_ref[0, row], jnp.int32)
            for m in range(1, K):
                line = jnp.where(lane == m, slots_ref[m, row], line)
            pc_send[side, j : j + 1, :] = line

    load_a.wait()
    first_tiles(a_v, t_own, lists_ref, s0_send)
    pl.semaphore_wait(barrier, 6)

    early = []
    for send, halo, ssem, rsem in (
        (t_send, None, t_ssem, t_rsem), (pc_send, pc_halo, pc_ssem, pc_rsem), (s0_send, s0_halo, s0_ssem, s0_rsem),
    ):
        for region, device in ((0, to_up), (1, to_down)):
            target = t_ext.at[pl.ds(TR + GD * region, GD)] if halo is None else halo.at[region]
            early.append(remote(send.at[1 - region], target, ssem.at[region], rsem.at[region], device))
            early[-1].start()

    clear_rows(p_all)
    load_ext.wait()
    load_cols.wait()
    early[0].wait_recv()
    early[1].wait_recv()

    def start_pair(side, pair):
        remote(
            s_send.at[0, side, pair], s_halo.at[0, 1 - side, pair], s_ssem.at[0, side], s_rsem.at[0, side],
            to_up if side == 1 else to_down,
        ).start()

    send_rows(a_v, t_ext, cols_ref, lists_ref, s_send, start_pair)

    def side_copy(half, side):
        return remote(
            s_send.at[half, side], s_halo.at[half, 1 - side], s_ssem.at[half, side], s_rsem.at[half, side],
            to_up if side == 1 else to_down,
        )

    s_copies = [[side_copy(half, side) for side in range(2)] for half in range(2)]

    place_of = [
        jnp.where(t == xa, 0, jnp.where(t == xb, 1, jnp.where(t == xo, 2, 3))) for t in range(4)
    ]
    own_rows(a_v, t_ext, cols_ref, slots_ref, p_all, p_t, place_of)
    for copy in s_copies[1]:
        copy.start()

    core_copies, x_copies, y_copies = [], [None] * 15, []

    def begin(copies, *args):
        copies.append(remote(*args))
        copies[-1].start()

    def core_stage(n):
        core_copies[n].wait_recv()
        for t in (2, 0, 1):
            encode(part[n, core, t] + core_in[n, t], x_out.at[n, t])
        for t in (2, 0, 1):
            i = 3 * n + t
            x_copies[i] = remote(x_out.at[n, t], x_in.at[n, t], x_ssem.at[i], x_rsem.at[i], to_ring[t])
            x_copies[i].start()
        q[n] = part[n, core, 3] + core_in[n, 3]

    def x_stage(n):
        for t in range(3):
            x_copies[3 * n + t].wait_recv()
        total = (q[n] + decode(x_in.at[n, 0])) + (decode(x_in.at[n, 1]) + decode(x_in.at[n, 2]))
        fin[1, n], fin[2, n], fin[0, n] = total[:32], total[32:64], total[64:]

    def y_stage(first, count):
        chunks = pl.ds(first, count)
        for region, device in ((0, to_up), (1, to_down)):
            i = 2 * first + region
            begin(
                y_copies, fin.at[region, chunks], y_in.at[region, chunks], y_ssem.at[i], y_rsem.at[i], device
            )

    def place(n):
        place_chunk(n, a_v, cols_ref, p_all, ap)

    def product(n):
        for c in range(2):
            product_chunk(n, c, p_t, ap, part)
        begin(core_copies, part.at[n, 1 - core], core_in.at[n], c_ssem.at[n], c_rsem.at[n], to_core)

    for copy in early[2:] + s_copies[0]:
        copy.wait_recv()
    halo_rows(0, s0_halo, s_halo, pc_halo, p_all)
    place(0)
    product(0)
    place(1)
    core_stage(0)
    product(1)
    for copy in s_copies[1]:
        copy.wait_recv()
    halo_rows(1, s0_halo, s_halo, pc_halo, p_all)
    place(2)
    core_stage(1)
    product(2)
    place(3)
    core_stage(2)
    product(3)
    place(4)
    core_stage(3)
    product(4)
    x_stage(0)
    core_stage(4)
    x_stage(1)
    x_stage(2)
    x_stage(3)
    y_stage(0, 4)
    x_stage(4)
    y_stage(4, 1)
    for copy in early + s_copies[0] + s_copies[1] + core_copies + x_copies + y_copies:
        copy.wait_send()
    for copy in y_copies:
        copy.wait_recv()

    def columns(array, half, group):
        chunk, at = chunk_of(half, group)
        return array(chunk)[:, at * B : (at + 1) * B]

    for g in range(7):
        halves = []
        for half in range(2):
            total = None
            for group, array in (
                (g - 1, lambda n: fin[2, n]),
                (g, lambda n: jnp.where(dom > 0, y_in[0, n], 0.0)),
                (g - 2, lambda n: jnp.where(dom < n_dom - 1, y_in[1, n], 0.0)),
            ):
                if 0 <= group < 5:
                    value = columns(array, half, group)
                    total = value if total is None else total + value
            halves.append(total)
        for s in range(2):
            out_ref[:, g * G + s * B : g * G + (s + 1) * B] = paired(halves[0], halves[1], s)


def on_device(a_vals, a_cols, send_rows, tentative, p_cols, ap_cols):
    hbm = pl.BlockSpec(memory_space=pl.ANY)
    dma = pltpu.SemaphoreType.DMA
    return pl.pallas_call(
        kernel,
        out_shape=jax.ShapeDtypeStruct((32, 7 * G), F32),
        in_specs=[hbm] * 5,
        out_specs=pl.BlockSpec(memory_space=pltpu.VMEM),
        scratch_shapes=[
            pltpu.SMEM((K, TR), jnp.int32), pltpu.SMEM((2, GD), jnp.int32), pltpu.SMEM((K, TR), jnp.int32),
            pltpu.VMEM((TR, K, B, B), BF16),
            pltpu.VMEM((TR, B, B), BF16),
            pltpu.VMEM((TR + 2 * GD, B, B), BF16),
            pltpu.VMEM((2, GD, B, B), BF16),
            pltpu.VMEM((2, GD, B, B), BF16),
            pltpu.VMEM((2, GD, B, B), BF16),
            pltpu.VMEM((2, 2, GD // 2, K - 1, B, B), BF16),
            pltpu.VMEM((2, 2, GD // 2, K - 1, B, B), BF16),
            pltpu.VMEM((2, GD, B), jnp.int32),
            pltpu.VMEM((2, GD, B), jnp.int32),
            pltpu.VMEM((TR + 2 * GD, 5, B, G), BF16),
            pltpu.VMEM((2, 4, R3, TR * B), BF16),
            pltpu.VMEM((5, TR * B, G), BF16),
            pltpu.VMEM((5, 2, 4, R3, G), F32),
            pltpu.VMEM((5, 4, R3, G), F32),
            pltpu.VMEM((5, R3, G), F32),
            pltpu.VMEM((5, 3, R3 + 16, G), jnp.int16),
            pltpu.VMEM((5, 3, R3 + 16, G), jnp.int16),
            pltpu.VMEM((3, 5, 32, G), F32),
            pltpu.VMEM((2, 5, 32, G), F32),
            dma((6,)),
            dma((2,)), dma((2,)), dma((2,)), dma((2,)), dma((2, 2)), dma((2, 2)), dma((2,)), dma((2,)),
            dma((5,)), dma((5,)), dma((15,)), dma((15,)), dma((10,)), dma((10,)),
        ],
        compiler_params=pltpu.CompilerParams(
            collective_id=0, has_side_effects=True, vmem_limit_bytes=60 * 1024 * 1024
        ),
        cost_estimate=pl.CostEstimate(flops=16_000_000_000, bytes_accessed=8_000_000, transcendentals=0),
    )(a_vals, a_cols.T, send_rows.reshape(2, GD), tentative, p_cols.T)


def solution(mesh):
    placed = (
        P(("dom", "sub"), None, None, None),
        P(("dom", "sub"), None),
        P(("dom", "sub"), None, None),
        P(("dom", "sub"), None, None),
        P(("dom", "sub"), None),
        P(("dom", "sub"), None, None),
    )
    return jax.shard_map(
        on_device, mesh=mesh, in_specs=placed, out_specs=P(("dom", "sub"), None), check_vma=False
    )
```
